256 devices in a mesh: item: 8 (over z), tensor: 32 (over x, y, core).
Axes of the slice: x: 4, y: 4, z: 8, core: 2. Of those that a mesh axis runs over, the one named last changes fastest.
Arguments:
- gated_hidden_input: bfloat16 [6144, 14336], P('item', 'tensor'), may hold values from -6 to 6
- residual_stream_input: bfloat16 [6144, 8192], P('item', 'tensor'), may hold values from -6 to 6
- down_matrix: bfloat16 [14336, 8192], P('tensor'), may hold values from -0.046875 to 0.046875
- adapter_input_factor: bfloat16 [16, 14336], P(None, 'tensor'), may hold values from -0.046875 to 0.046875
- adapter_output_factor: bfloat16 [16, 8192], P(None, 'tensor'), may hold values from -1.5 to 1.5
- final_norm_scale: bfloat16 [8192], P('tensor'), may hold values from 0.5 to 1.5
- answer_head_rows: bfloat16 [4, 8192], P(None, 'tensor'), may hold values from -0.0625 to 0.0625
- answer_prior_offsets: float32 [6144, 4], P('item'), may hold values from -320 to 320
- input_factor_direction: bfloat16 [2, 16, 14336], P(None, None, 'tensor'), may hold values from -6 to 6
- output_factor_direction: bfloat16 [2, 16, 8192], P(None, None, 'tensor'), may hold values from -1.5 to 1.5
Outputs:
- ggn_a: float32 [2, 16, 14336], P(None, None, 'tensor')
- curvature_output_parts: float32 [2, 16, 8192], P(None, None, 'tensor')
The draws below stay inside these ranges and needn't reach their ends.
All inputs are finite; a program needn't handle non-finite values.
Results may differ from the reference program's by a relative error of at most 0.0003.
Values may be sent and summed in bfloat16 or wider, within the bound.
A program may use at most 128 MiB of HBM per device.

```python
import jax
import jax.numpy as jnp
from jax import lax

MODEL_DIM = 8192
FEEDFWD_WIDTH = 14336
ADAPTER_RANK = 16
CLASSES = 4
K = 2
TOKENS = 6144
N_TENSOR = 32


def draw_answer_prior_offsets(key, part):
    key = jax.random.fold_in(key, 7)
    key_base = jax.random.fold_in(key, 0)
    base = 2.0 * jax.random.normal(key_base, (TOKENS, CLASSES), jnp.float32)
    return base


def level_of(key, shape, cuts, low, high):
    factor_of, own = 1.0, jax.random.fold_in(key, 6)
    for axis_at, shards_of in cuts:
        heights = jnp.exp(jax.random.uniform(jax.random.fold_in(own, axis_at), (shards_of,), jnp.float32, low / len(cuts), high / len(cuts)))
        factor_of = factor_of * jnp.repeat(heights, shape[axis_at] // shards_of).reshape([-1 if axis == axis_at else 1 for axis in range(len(shape))])
    return factor_of


def normal_values(key, extent, scale, most, cuts=(), kind=jnp.bfloat16):
    level = level_of(key, extent, cuts, -0.22, 0.18) if cuts else 1.0
    entries = jax.random.normal(key, extent, jnp.float32) * scale * level
    return jnp.minimum(jnp.maximum(entries, -most), most).astype(kind)


def setup_inputs(seed: int = 0) -> dict:
    keys = jax.random.split(jax.random.key(seed), 11)
    gated_hidden_input = normal_values(keys[0], (TOKENS, FEEDFWD_WIDTH), 1.0, 6.0, ((0, 8), (1, 32)))
    residual_stream_input = normal_values(keys[1], (TOKENS, MODEL_DIM), 1.0, 6.0, ((0, 8), (1, 32)))
    down_matrix = normal_values(keys[2], (FEEDFWD_WIDTH, MODEL_DIM), FEEDFWD_WIDTH ** -0.5, 0.046875, ((0, 32),))
    adapter_input_factor = normal_values(keys[3], (ADAPTER_RANK, FEEDFWD_WIDTH), FEEDFWD_WIDTH ** -0.5, 0.046875, ((1, 32),))
    adapter_output_factor = normal_values(keys[4], (ADAPTER_RANK, MODEL_DIM), ADAPTER_RANK ** -0.5, 1.5, ((1, 32),))
    final_norm_scale = jnp.clip(1.0 + 0.1 * jax.random.normal(keys[5], (MODEL_DIM,), jnp.float32), 0.5, 1.5).astype(jnp.bfloat16)
    answer_head_rows = normal_values(keys[6], (CLASSES, MODEL_DIM), MODEL_DIM ** -0.5, 0.0625, ((1, 32),))
    answer_prior_offsets = draw_answer_prior_offsets(jax.random.fold_in(keys[10], 71), 0)
    input_factor_direction = normal_values(keys[8], (K, ADAPTER_RANK, FEEDFWD_WIDTH), 1.0, 6.0, ((2, 32),))
    output_factor_direction = normal_values(keys[9], (K, ADAPTER_RANK, MODEL_DIM), 0.25, 1.5, ((2, 32),))
    return dict(gated_hidden_input=gated_hidden_input, residual_stream_input=residual_stream_input, down_matrix=down_matrix, adapter_input_factor=adapter_input_factor, adapter_output_factor=adapter_output_factor, final_norm_scale=final_norm_scale, answer_head_rows=answer_head_rows, answer_prior_offsets=answer_prior_offsets, input_factor_direction=input_factor_direction, output_factor_direction=output_factor_direction)


ADAPTER_SCALE = 2.0
EPS = 1e-05

def reference(gated_hidden_input, residual_stream_input, down_matrix, adapter_input_factor, adapter_output_factor, final_norm_scale, answer_head_rows, answer_prior_offsets, input_factor_direction, output_factor_direction):
    block_ff = FEEDFWD_WIDTH // N_TENSOR
    block_d = MODEL_DIM // N_TENSOR
    highest_precision = lax.Precision.HIGHEST

    def add_block(total, index):
        xs = lax.dynamic_slice_in_dim(gated_hidden_input, index * block_ff, block_ff, 1)
        ws = lax.dynamic_slice_in_dim(down_matrix, index * block_ff, block_ff, 0)
        term = jnp.dot(xs, ws, preferred_element_type=jnp.float32)
        res = lax.dynamic_slice_in_dim(residual_stream_input, index * block_d, block_d, 1).astype(jnp.float32)
        old = lax.dynamic_slice_in_dim(term, index * block_d, block_d, 1)
        term = lax.dynamic_update_slice_in_dim(term, old + res, index * block_d, 1)
        return (total + term, None)
    summed_parts, _ = lax.scan(add_block, jnp.zeros((TOKENS, MODEL_DIM), jnp.float32), jnp.arange(N_TENSOR, dtype=jnp.int32))
    x_wide = gated_hidden_input.astype(jnp.float32)
    input_times_factor = jnp.dot(gated_hidden_input, adapter_input_factor.T, preferred_element_type=jnp.float32)
    input_times_direction = jnp.einsum('tf,krf->ktr', x_wide, input_factor_direction.astype(jnp.float32), precision=highest_precision)
    output_factor = adapter_output_factor.astype(jnp.float32)
    direction_wide_matrix = output_factor_direction.astype(jnp.float32)
    gain = final_norm_scale.astype(jnp.float32)
    head = answer_head_rows.astype(jnp.float32)
    hidden_state = summed_parts + ADAPTER_SCALE * jnp.dot(input_times_factor, output_factor, precision=highest_precision)
    hidden_delta = ADAPTER_SCALE * (jnp.einsum('aqe,eu->aqu', input_times_direction, output_factor, precision=highest_precision) + jnp.einsum('gs,ysp->ygp', input_times_factor, direction_wide_matrix, precision=highest_precision))
    rank_index = lax.rsqrt(lax.optimization_barrier(jnp.mean(hidden_state * hidden_state, axis=1, keepdims=True)) + EPS)
    m = lax.optimization_barrier(jnp.mean(hidden_state[None] * hidden_delta, axis=2, keepdims=True))
    logits = jnp.dot(hidden_state * rank_index * gain, head.T, precision=highest_precision) + answer_prior_offsets
    p = jax.nn.softmax(logits, axis=1)
    dn = gain * (hidden_delta * rank_index - hidden_state * rank_index ** 3 * m)
    dl = jnp.einsum('ktd,cd->ktc', dn, head, precision=highest_precision)
    q = p * (dl - lax.optimization_barrier(jnp.sum(p * dl, axis=2, keepdims=True))) / TOKENS
    gbar = gain * jnp.einsum('ktc,cd->ktd', q, head, precision=highest_precision)
    probability_weights = lax.optimization_barrier(jnp.mean(hidden_state * gbar, axis=2, keepdims=True))
    mean_hidden = rank_index * gbar - hidden_state * rank_index ** 3 * probability_weights
    curvature_output_parts = ADAPTER_SCALE * jnp.einsum('cf,mce->mfe', input_times_factor, mean_hidden, precision=highest_precision)
    direction_output = ADAPTER_SCALE * jnp.einsum('mjb,pb->mjp', mean_hidden, output_factor, precision=highest_precision)
    ggn_a = jnp.einsum('ktr,tf->krf', direction_output, x_wide, precision=highest_precision)
    return (ggn_a, curvature_output_parts)
```

```python
import jax
import jax.numpy as jnp
from jax import lax
from jax.sharding import PartitionSpec as P

SCALE = 2.0
EPS = 1e-05
HI = lax.Precision.HIGHEST


def split3(v):
    a = lax.reduce_precision(v, 8, 7)
    b = lax.reduce_precision(v - a, 8, 7)
    c = v - a - b
    return tuple(part.astype(jnp.bfloat16) for part in (a, b, c))


def shards(x, res, w, a_in, b_out, gain, head, prior, v_in, d_out):
    f32 = jnp.float32
    width = lax.axis_size("tensor")
    rows, piece = x.shape
    rank = a_in.shape[0]
    k = v_in.shape[0]
    model = w.shape[1]
    total_rows = rows * lax.axis_size("item")
    gh = gain.astype(f32)[None] * head.astype(f32)
    g_hi, g_lo, _ = split3(gh)
    classes = head.shape[0]
    proj = jnp.concatenate([b_out, d_out.reshape(k * rank, -1), g_hi, g_lo], 0)
    full = lax.all_gather(proj, "tensor", axis=1, tiled=True)
    y = lax.dot_general(w, full, (((1,), (1,)), ((), ())), preferred_element_type=f32)
    gram = lax.dot_general(full, full, (((1,), (1,)), ((), ())), preferred_element_type=f32)
    av = jnp.concatenate([a_in[None], v_in], 0).reshape((k + 1) * rank, piece)
    low = lax.dot_general(x, av, (((1,), (1,)), ((), ())), preferred_element_type=f32)
    hp = lax.dot_general(res, proj, (((1,), (1,)), ((), ())), preferred_element_type=f32)
    for part in split3(y):
        hp = hp + jnp.dot(x, part, preferred_element_type=f32)
    low = lax.psum(jnp.concatenate([low, hp], 1), "tensor")
    term = jnp.dot(x, w, preferred_element_type=f32).astype(jnp.bfloat16)
    summed = lax.psum_scatter(term, "tensor", scatter_dimension=1, tiled=True).astype(f32)

    xa = low[:, :rank]
    xv = [low[:, rank * (i + 1):rank * (i + 2)] for i in range(k)]
    hp = low[:, rank * (k + 1):] + SCALE * jnp.dot(xa, gram[:rank], precision=HI)
    n = rank * (k + 1)

    def fold(m):
        return jnp.concatenate([m[..., :n], m[..., n:n + classes] + m[..., n + classes:]], -1)

    hp = fold(hp)
    gram = fold(fold(gram).T).T
    h = summed + res.astype(f32) + SCALE * jnp.dot(xa, b_out.astype(f32), precision=HI)
    sq = lax.psum(jnp.sum(h * h, 1), "tensor")
    r = lax.rsqrt(sq / model + EPS)[:, None]
    hg = hp[:, n:]
    hb = hp[:, :rank]
    logits = r * hg + prior
    top = jnp.max(logits, axis=1, keepdims=True)
    ex = jnp.exp(logits - top)
    p = ex / jnp.sum(ex, axis=1, keepdims=True)
    us, cs, qs = [], [], []
    for i in range(k):
        lo, hi_ = rank * (i + 1), rank * (i + 2)
        m = SCALE * jnp.sum(xv[i] * hb + xa * hp[:, lo:hi_], 1, keepdims=True) / model
        dhg = SCALE * (jnp.dot(xv[i], gram[:rank, n:], precision=HI) + jnp.dot(xa, gram[lo:hi_, n:], precision=HI))
        dl = r * dhg - r**3 * m * hg
        q = p * (dl - jnp.sum(p * dl, 1, keepdims=True)) / total_rows
        s = jnp.sum(q * hg, 1, keepdims=True) / model
        us.append(SCALE * (r * jnp.dot(q, gram[n:, :rank], precision=HI) - r**3 * s * hb))
        cs.append(r**3 * s * xa)
        qs.append(r * q)
    u = jnp.concatenate(us, 1)
    c = jnp.concatenate(cs, 1)
    q = jnp.concatenate(qs, 1)
    ggn = 0.0
    for part in split3(u):
        ggn = ggn + lax.dot_general(part, x, (((0,), (0,)), ((), ())), preferred_element_type=f32)
    t1 = lax.dot_general(q, xa, (((0,), (0,)), ((), ())), precision=HI).reshape(k, classes, rank)
    curv = SCALE * (
        jnp.einsum("kce,cd->ked", t1, gh, precision=HI).reshape(k * rank, -1)
        - lax.dot_general(c, h, (((0,), (0,)), ((), ())), precision=HI)
    )
    out = lax.psum(jnp.concatenate([ggn, curv], 1), "item")
    return out[:, :piece].reshape(k, rank, piece), out[:, piece:].reshape(k, rank, -1)


def solution(mesh):
    placed = (
        P("item", "tensor"),
        P("item", "tensor"),
        P("tensor", None),
        P(None, "tensor"),
        P(None, "tensor"),
        P("tensor"),
        P(None, "tensor"),
        P("item", None),
        P(None, None, "tensor"),
        P(None, None, "tensor"),
    )
    return jax.shard_map(
        shards,
        mesh=mesh,
        in_specs=placed,
        out_specs=(P(None, None, "tensor"), P(None, None, "tensor")),
        check_vma=False,
    )
```

```python
import functools

import jax
import jax.numpy as jnp
from jax import lax
from jax.experimental import pallas as pl
from jax.experimental.pallas import tpu as pltpu
from jax.sharding import PartitionSpec as P

SCALE = 2.0
EPS = 1e-05
HI = lax.Precision.HIGHEST
F32 = jnp.float32
BF16 = jnp.bfloat16
N = 4
NT = (((1,), (1,)), ((), ()))
NN = (((1,), (0,)), ((), ()))


def dot(a, b, dims=NN, precision=None):
    return lax.dot_general(a, b, dims, preferred_element_type=F32, precision=precision)


def split3(v):
    a = v.astype(BF16)
    rest = v - a.astype(F32)
    b = rest.astype(BF16)
    c = (rest - b.astype(F32)).astype(BF16)
    return a, b, c


def wrap(v):
    return lax.rem(v, N)


def kernel(
    chunks, zs, total_tokens,
    x_hbm, r_hbm, w_hbm, a_ref, b_ref, g_ref, head_ref, prior_ref, v_ref, d_ref,
    ggn_ref, curv_ref,
    xbuf, rbuf, wbuf, tb, r1, r2, pf, g8, avp, ybuf, gram, lbuf, la, lc, lx, ly, lfull,
    hhi, hlo, ssend, sx, sy, sc, zpart, zrecv, zfull,
    wl, xl, rl, ws, wr, xs, xr, ms, mr, ns, nr, c1s, c1r, c2s, c2r, c3s, c3r, zss, zsr,
):
    rows, piece = x_hbm.shape
    half = rows // 2
    tc = half // chunks
    fb = r_hbm.shape[1]
    lanes = 128
    model = w_hbm.shape[1]
    rank = a_ref.shape[0]
    zi = lax.axis_index("item")
    me = lax.axis_index("tensor")
    core = lax.rem(me, 2)
    chip = lax.div(me, 2)
    px = lax.div(chip, N)
    py = lax.rem(chip, N)

    def device(x, y, c):
        return {"tensor": (x * N + y) * 2 + c}

    sibling = device(px, py, 1 - core)
    xpeer = [None] + [device(wrap(px + o), py, core) for o in range(1, N)]
    ypeer = [None] + [device(px, wrap(py + o), core) for o in range(1, N)]
    zpeer = [None] + [{"item": lax.rem(zi + o, zs)} for o in range(1, zs)]
    sends = []

    def send(src, dst, ssem, rsem, to):
        copy = pltpu.make_async_remote_copy(
            src_ref=src, dst_ref=dst, send_sem=ssem, recv_sem=rsem,
            device_id=to, device_id_type=pl.DeviceIdType.MESH,
        )
        copy.start()
        sends.append(copy)
        return copy

    order = [(2, o) for o in range(N)] + [(o, 2) for o in (0, 1, 3)]
    order += [(i, j) for i in (1, 3, 0) for j in (1, 3, 0)]

    def block(n):
        return wrap(px + order[n][0]) * N + wrap(py + order[n][1])

    def columns(b, c):
        return pl.ds(pl.multiple_of((b * 2 + c) * fb, fb), fb)

    xloads = [
        pltpu.make_async_copy(x_hbm.at[pl.ds(f * half, half)], xbuf.at[0, pl.ds(f * half, half)], xl.at[f])
        for f in range(2)
    ]
    wloads = [
        pltpu.make_async_copy(w_hbm.at[:, columns(block(n), core)], wbuf.at[0, block(n)], wl.at[n])
        for n in range(N * N)
    ]
    rload = pltpu.make_async_copy(r_hbm, rbuf, rl.at[0])
    xloads[0].start()
    for n in range(N):
        wloads[n].start()
    xloads[1].start()
    for n in range(N, N * N):
        wloads[n].start()
    rload.start()

    g8[...] = jnp.zeros_like(g8)
    g8[0:4, :] = head_ref[...].astype(F32) * g_ref[...].astype(F32)
    ghi = g8[...].astype(BF16).astype(F32)
    pf[:, :, 64:128, :] = jnp.zeros((N, N, 64, fb), BF16)
    pf[py, px, 0:rank, :] = b_ref[...]
    pf[py, px, rank:3 * rank, :] = d_ref[...]
    pf[py, px, 3 * rank:64, :] = jnp.concatenate([ghi, g8[...] - ghi], 0).astype(BF16)
    avp[...] = jnp.zeros_like(avp)
    avp[64:64 + rank, :] = a_ref[...]
    avp[64 + rank:64 + 3 * rank, :] = v_ref[...]

    barrier = pltpu.get_barrier_semaphore()
    peers = [sibling] + xpeer[1:] + ypeer[1:] + zpeer[1:]
    for to in peers:
        pl.semaphore_signal(barrier, inc=1, device_id=to, device_id_type=pl.DeviceIdType.MESH)
    pl.semaphore_wait(barrier, len(peers))

    def send_x(f):
        return send(x_hbm.at[pl.ds(f * half, half)], xbuf.at[1, pl.ds(f * half, half)], xs.at[f], xr.at[f], sibling)

    def send_w(n):
        return send(w_hbm.at[:, columns(block(n), 1 - core)], wbuf.at[1, block(n)], ws.at[n], wr.at[n], sibling)

    xin = [send_x(0)]
    win = [send_w(n) for n in range(N)]
    pin = [
        send(pf.at[py, px, pl.ds(0, 64)], pf.at[py, px, pl.ds(0, 64)], c1s.at[0, o - 1], c1r.at[0, o - 1], xpeer[o])
        for o in range(1, N)
    ]
    xin.append(send_x(1))
    win += [send_w(n) for n in range(N, N * N)]

    def recv_slot(src_shape_ref, sem):
        return pltpu.make_async_copy(src_shape_ref, src_shape_ref, sem)

    pos = [(px, py), (py, px)]

    def group(f, i1):
        def body(i2, carry):
            b = i1 * N + i2 if f == 0 else i2 * N + i1
            acc = dot(xbuf[0, f * half:(f + 1) * half, :], wbuf[0, b])
            acc = acc + dot(xbuf[1, f * half:(f + 1) * half, :], wbuf[1, b])
            out = acc.astype(BF16)
            tb[f, i1 * N + i2, 0] = out[:, :lanes]
            tb[f, i1 * N + i2, 1] = out[:, lanes:]
            return carry

        lax.fori_loop(0, N, body, 0)

    def step1(f, o):
        p1 = wrap(pos[f][0] + o)
        peer = xpeer if f == 0 else ypeer
        return p1, peer

    def send_m(f, c, direction, msg):
        peer = xpeer if f == 0 else ypeer
        to = peer[1] if direction == 0 else peer[N - 1]
        offset = 2 if msg == 0 else (1 if direction == 0 else N - 1)
        i1 = wrap(pos[f][0] + offset)
        part = 1 - direction if msg == 1 else direction
        send(
            tb.at[f, pl.ds(i1 * N + 2 * part, 2), :, pl.ds(c * tc, tc), :],
            r1.at[f, c, direction, msg],
            ms.at[f, c, direction, msg], mr.at[f, c, direction, msg], to,
        )

    def wait_m(f, c, direction, msg):
        recv_slot(r1.at[f, c, direction, msg], mr.at[f, c, direction, msg]).wait()

    def send_n(f, c, direction, msg):
        peer = ypeer if f == 0 else xpeer
        to = peer[1] if direction == 0 else peer[N - 1]
        offset = 2 if msg == 0 else (1 if direction == 0 else N - 1)
        i2 = wrap(pos[f][1] + offset)
        part = 1 - direction if msg == 1 else direction
        send(
            tb.at[f, pos[f][0] * N + i2, part, pl.ds(c * tc, tc), :],
            r2.at[f, c, direction, msg],
            ns.at[f, c, direction, msg], nr.at[f, c, direction, msg], to,
        )

    def wait_n(f, c, direction, msg):
        recv_slot(r2.at[f, c, direction, msg], nr.at[f, c, direction, msg]).wait()

    def wait_w(n):
        wloads[n].wait()
        win[n].wait_recv()

    xloads[0].wait()
    xin[0].wait_recv()
    for n in range(N):
        wait_w(n)
    group(0, wrap(px + 2))
    for c in range(chunks):
        for direction in range(2):
            send_m(0, c, direction, 0)
    for copy in pin:
        copy.wait_recv()
    pin2 = [
        send(pf.at[py, :, pl.ds(0, 64)], pf.at[py, :, pl.ds(0, 64)], c1s.at[1, o - 1], c1r.at[1, o - 1], ypeer[o])
        for o in range(1, N)
    ]
    xloads[1].wait()
    xin[1].wait_recv()
    for n in range(N, 2 * N - 1):
        wait_w(n)
    group(1, wrap(py + 2))
    for c in range(chunks):
        for direction in range(2):
            send_m(1, c, direction, 0)
    for n in range(2 * N - 1, N * N):
        wait_w(n)
    for f in range(2):
        group(f, wrap(pos[f][0] + 1))
        group(f, wrap(pos[f][0] + N - 1))
        for c in range(chunks):
            for direction in range(2):
                send_m(f, c, direction, 1)

    def middle(f, c):
        for direction in range(2):
            wait_m(f, c, direction, 0)
            i1 = wrap(pos[f][0] + (1 if direction == 0 else N - 1))
            at = (f, pl.ds(i1 * N + 2 * direction, 2), slice(None), pl.ds(c * tc, tc), slice(None))
            tb[at] = (tb[at].astype(F32) + r1[f, c, direction, 0].astype(F32)).astype(BF16)
            send_m(f, c, direction, 2)

    for f in range(2):
        group(f, pos[f][0])
    for c in range(chunks):
        for f in range(2):
            middle(f, c)

    for copy in pin2:
        copy.wait_recv()
    eye = (
        lax.broadcasted_iota(jnp.int32, (piece, piece), 0) == lax.broadcasted_iota(jnp.int32, (piece, piece), 1)
    ).astype(F32).astype(BF16)
    ybuf[0] = dot(eye, avp[...], NT)
    ybuf[1] = jnp.zeros((piece, lanes), F32)
    gram[0] = jnp.zeros((64, lanes), F32)

    def project(b, carry):
        i, j = lax.div(b, N), lax.rem(b, N)
        p = pf[j, i]
        ybuf[0] = ybuf[0] + dot(wbuf[0, b], p, NT)
        ybuf[1] = ybuf[1] + dot(wbuf[1, b], p, NT)
        gram[0] = gram[0] + dot(p[0:64], p, NT)
        return carry

    lax.fori_loop(0, N * N, project, 0)
    rload.wait()
    for s in range(2):
        for i, part in enumerate(split3(ybuf[s])):
            yi = part
            for f in range(2):
                at = slice(f * half, (f + 1) * half)
                add = dot(xbuf[s, at, :], yi)
                if s == 0 and i == 0:
                    lbuf[at, :] = dot(rbuf[at, :], pf[py, px], NT) + add
                else:
                    lbuf[at, :] = lbuf[at, :] + add
    other = pl.multiple_of((1 - core) * half, half)
    mine = pl.multiple_of(core * half, half)
    lin = send(lbuf.at[pl.ds(other, half)], la, c2s.at[0], c2r.at[0], sibling)
    gin = send(gram.at[0], gram.at[1], c2s.at[1], c2r.at[1], sibling)

    def stage2(f, c):
        wait_m(f, c, 0, 1)
        wait_m(f, c, 1, 1)
        wait_m(f, c, 0, 2)
        wait_m(f, c, 1, 2)
        for part in range(2):
            at = (f, pl.ds(pos[f][0] * N + 2 * part, 2), slice(None), pl.ds(c * tc, tc), slice(None))
            tb[at] = (
                tb[at].astype(F32)
                + r1[f, c, part, 2].astype(F32)
                + r1[f, c, 1 - part, 1].astype(F32)
            ).astype(BF16)
        for msg in range(2):
            for direction in range(2):
                send_n(f, c, direction, msg)

    def stage3(f, c):
        for direction in range(2):
            wait_n(f, c, direction, 0)
            i2 = wrap(pos[f][1] + (1 if direction == 0 else N - 1))
            at = (f, pos[f][0] * N + i2, direction, pl.ds(c * tc, tc), slice(None))
            tb[at] = (tb[at].astype(F32) + r2[f, c, direction, 0].astype(F32)).astype(BF16)
            send_n(f, c, direction, 2)

    lin.wait_recv()
    lc[...] = lbuf[pl.ds(mine, half), :] + la[...]
    q1, q2 = half // N, half // N // N

    def xslice(o):
        return pl.ds(pl.multiple_of(wrap(px + o) * q1, q1), q1)

    bins = [send(lc.at[xslice(o)], lx.at[o - 1], c2s.at[1 + o], c2r.at[1 + o], xpeer[o]) for o in range(1, N)]
    for f in range(2):
        stage2(f, 0)
    for copy in bins:
        copy.wait_recv()
    lc[xslice(0), :] = lc[xslice(0), :] + lx[0] + lx[1] + lx[2]

    def yslice(o):
        return pl.ds(pl.multiple_of(px * q1 + wrap(py + o) * q2, q2), q2)

    cins = [send(lc.at[yslice(o)], ly.at[o - 1], c2s.at[4 + o], c2r.at[4 + o], ypeer[o]) for o in range(1, N)]
    for f in range(2):
        stage3(f, 0)
        stage2(f, 1)
    for copy in cins:
        copy.wait_recv()
    lfull[core, px, py] = lc[yslice(0), :] + ly[0] + ly[1] + ly[2]
    own = lfull.at[core, px, py]
    dins = [send(own, own, c2s.at[7 + o], c2r.at[7 + o], ypeer[o]) for o in range(1, N)]
    for f in range(2):
        stage3(f, 1)
    for copy in dins:
        copy.wait_recv()
    own = lfull.at[core, px]
    eins = [send(own, own, c2s.at[10 + o], c2r.at[10 + o], xpeer[o]) for o in range(1, N)]
    for f in range(2):
        stage2(f, 2)
    for copy in eins:
        copy.wait_recv()
    own = lfull.at[core]
    fin = send(own, own, c2s.at[14], c2r.at[14], sibling)
    for f in range(2):
        stage3(f, 2)
    fin.wait_recv()
    gin.wait_recv()

    low = lfull[...].reshape(rows, lanes)
    lt = low.T
    gm = (gram[0] + gram[1])[:, 0:64]
    xa = lt[64:64 + rank]
    xv = [lt[64 + rank * (i + 1):64 + rank * (i + 2)] for i in range(2)]
    zero16 = jnp.zeros((rank, rows), F32)
    hp = lt[0:64] + SCALE * dot(gm, jnp.concatenate([xa, zero16, zero16, zero16], 0), precision=HI)
    hb = hp[0:rank]
    hg = hp[48:56] + hp[56:64]
    gm8 = gm[48:56] + gm[56:64]
    stacks = [
        jnp.concatenate([xv[0], xa, zero16, zero16], 0),
        jnp.concatenate([xv[1], zero16, xa, zero16], 0),
    ]
    dhg = [SCALE * dot(gm8, st, precision=HI) for st in stacks]
    mk = [
        SCALE / model * jnp.sum(xv[i] * hb + xa * hp[rank * (i + 1):rank * (i + 2)], 0, keepdims=True)
        for i in range(2)
    ]
    pick = (
        lax.broadcasted_iota(jnp.int32, (8, 4), 0) == lax.broadcasted_iota(jnp.int32, (8, 4), 1)
    ).astype(F32)
    prior = dot(pick, prior_ref[...], NT, precision=HI)

    xa_cols = [part for part in split3(low)]
    shift = (
        lax.broadcasted_iota(jnp.int32, (lanes, rank), 0) == lax.broadcasted_iota(jnp.int32, (lanes, rank), 1) + 64
    ).astype(F32).astype(BF16)
    spread = dot(shift, b_ref[...]).astype(BF16)
    ssend[...] = jnp.zeros_like(ssend)
    for c in range(chunks):
        for f in range(2):
            for direction in range(2):
                wait_n(f, c, direction, 1)
                wait_n(f, c, direction, 2)
            at = slice(f * half + c * tc, f * half + (c + 1) * tc)
            ad = dot(xa_cols[0][at], spread) + dot(xa_cols[1][at], spread) + dot(xa_cols[2][at], spread)
            parts = []
            for part in range(2):
                parts.append(
                    tb[f, pos[f][0] * N + pos[f][1], part, c * tc:(c + 1) * tc, :].astype(F32)
                    + r2[f, c, part, 2].astype(F32)
                    + r2[f, c, 1 - part, 1].astype(F32)
                )
            h = jnp.concatenate(parts, 1) + rbuf[at, :].astype(F32) + SCALE * ad
            hi = h.astype(BF16)
            hhi[at, :] = hi
            hlo[at, :] = (h - hi.astype(F32)).astype(BF16)
            sq = h * h
            sq = sq[:, :lanes] + sq[:, lanes:]
            n = f * chunks + c
            ssend[n:n + 1, :] = jnp.sum(sq.T, 0, keepdims=True)

    ins = [send(ssend, sx.at[o - 1], c3s.at[o - 1], c3r.at[o - 1], xpeer[o]) for o in range(1, N)]
    for copy in ins:
        copy.wait_recv()
    sc[0] = ssend[...] + sx[0] + sx[1] + sx[2]
    ins = [send(sc.at[0], sy.at[o - 1], c3s.at[2 + o], c3r.at[2 + o], ypeer[o]) for o in range(1, N)]
    for copy in ins:
        copy.wait_recv()
    sc[1] = sc[0] + sy[0] + sy[1] + sy[2]
    send(sc.at[1], sc.at[2], c3s.at[6], c3r.at[6], sibling).wait_recv()
    stot = sc[1] + sc[2]
    square = jnp.concatenate([stot[i:i + 1, :] for i in range(2 * chunks)], 1)

    r = lax.rsqrt(square / model + EPS)
    r3 = r * r * r
    live = lax.broadcasted_iota(jnp.int32, (8, rows), 0) < 4
    logits = jnp.where(live, r * hg + prior, -1e30)
    ex = jnp.where(live, jnp.exp(logits - jnp.max(logits, 0, keepdims=True)), 0.0)
    p = ex / jnp.sum(ex, 0, keepdims=True)
    us, cs, t1 = [], [], []
    gcol = gm[0:rank]
    for i in range(2):
        dl = r * dhg[i] - r3 * mk[i] * hg
        q = p * (dl - jnp.sum(p * dl, 0, keepdims=True)) / total_tokens
        s = jnp.sum(q * hg, 0, keepdims=True) / model
        back = dot(gcol, jnp.concatenate([zero16, zero16, zero16, q, q], 0), precision=HI)
        us.append(SCALE * (r * back - r3 * s * hb))
        cs.append(r3 * s * xa)
        t1.append(dot(xa, r * q, NT, precision=HI))
    uu = jnp.concatenate(split3(jnp.concatenate(us, 0)), 0)
    cc = jnp.concatenate(split3(jnp.concatenate(cs, 0)), 0)
    n32 = 2 * rank

    def fold(m):
        return m[0:n32] + m[n32:2 * n32] + m[2 * n32:3 * n32]

    ggn = fold(dot(uu, xbuf[0]))
    ch = fold(dot(cc, hhi[...]) + dot(cc, hlo[...]))
    curv = SCALE * (dot(jnp.concatenate(t1, 0), g8[...], precision=HI) - ch)

    zw = 3 * lanes
    for i in range(4):
        at = slice(8 * i, 8 * i + 8)
        zpart[2 * i] = ggn[at, 0:zw]
        zpart[2 * i + 1, :, 0:piece - zw] = ggn[at, zw:piece]
        zpart[2 * i + 1, :, lanes:zw] = curv[at, :]
    ins = []
    for o in range(1, zs):
        ins.append(send(zpart.at[lax.rem(zi + o, zs)], zrecv.at[o - 1], zss.at[0, o - 1], zsr.at[0, o - 1], zpeer[o]))
    for copy in ins:
        copy.wait_recv()
    total = zpart[zi]
    for o in range(1, zs):
        total = total + zrecv[o - 1]
    zfull[zi] = total
    ins = [
        send(zfull.at[zi], zfull.at[zi], zss.at[1, o - 1], zsr.at[1, o - 1], zpeer[o]) for o in range(1, zs)
    ]
    for copy in ins:
        copy.wait_recv()
    for i in range(4):
        at = slice(8 * i, 8 * i + 8)
        ggn_ref[at, 0:zw] = zfull[2 * i]
        ggn_ref[at, zw:piece] = zfull[2 * i + 1, :, 0:piece - zw]
        curv_ref[at, :] = zfull[2 * i + 1, :, lanes:zw]
    for copy in sends:
        copy.wait_send()


def shards(zs, x, res, w, a_in, b_out, gain, head, prior, v_in, d_out):
    rows, piece = x.shape
    fb = res.shape[1]
    rank = a_in.shape[0]
    k = v_in.shape[0]
    chunks = 3
    half = rows // 2
    tc = half // chunks
    vmem = pl.BlockSpec(memory_space=pltpu.VMEM)
    hbm = pl.BlockSpec(memory_space=pl.ANY)
    dma = pltpu.SemaphoreType.DMA
    ggn, curv = pl.pallas_call(
        functools.partial(kernel, chunks, zs, rows * zs),
        out_shape=(
            jax.ShapeDtypeStruct((k * rank, piece), F32),
            jax.ShapeDtypeStruct((k * rank, fb), F32),
        ),
        in_specs=[hbm, hbm, hbm] + [vmem] * 7,
        out_specs=(vmem, vmem),
        scratch_shapes=[
            pltpu.VMEM((2, rows, piece), BF16),
            pltpu.VMEM((rows, fb), BF16),
            pltpu.VMEM((2, N * N, piece, fb), BF16),
            pltpu.VMEM((2, N * N, 2, half, 128), BF16),
            pltpu.VMEM((2, chunks, 2, 3, 2, 2, tc, 128), BF16),
            pltpu.VMEM((2, chunks, 2, 3, tc, 128), BF16),
            pltpu.VMEM((N, N, 128, fb), BF16),
            pltpu.VMEM((8, fb), F32),
            pltpu.VMEM((128, piece), BF16),
            pltpu.VMEM((2, piece, 128), F32),
            pltpu.VMEM((2, 64, 128), F32),
            pltpu.VMEM((rows, 128), F32),
            pltpu.VMEM((half, 128), F32),
            pltpu.VMEM((half, 128), F32),
            pltpu.VMEM((N - 1, half // N, 128), F32),
            pltpu.VMEM((N - 1, half // N // N, 128), F32),
            pltpu.VMEM((2, N, N, half // N // N, 128), F32),
            pltpu.VMEM((rows, fb), BF16),
            pltpu.VMEM((rows, fb), BF16),
            pltpu.VMEM((8, 128), F32),
            pltpu.VMEM((N - 1, 8, 128), F32),
            pltpu.VMEM((N - 1, 8, 128), F32),
            pltpu.VMEM((3, 8, 128), F32),
            pltpu.VMEM((8, 8, 384), F32),
            pltpu.VMEM((zs - 1, 8, 384), F32),
            pltpu.VMEM((8, 8, 384), F32),
            dma((N * N,)), dma((2,)), dma((1,)),
            dma((N * N,)), dma((N * N,)), dma((2,)), dma((2,)),
            dma((2, chunks, 2, 3)), dma((2, chunks, 2, 3)),
            dma((2, chunks, 2, 3)), dma((2, chunks, 2, 3)),
            dma((2, N - 1)), dma((2, N - 1)),
            dma((15,)), dma((15,)), dma((7,)), dma((7,)),
            dma((2, zs - 1)), dma((2, zs - 1)),
        ],
        compiler_params=pltpu.CompilerParams(
            collective_id=0, has_side_effects=True, vmem_limit_bytes=56 * 1024 * 1024
        ),
    )(
        x, res, w, a_in, b_out, gain.reshape(1, fb), head, prior,
        v_in.reshape(k * rank, piece), d_out.reshape(k * rank, fb),
    )
    return ggn.reshape(k, rank, piece), curv.reshape(k, rank, fb)


def solution(mesh):
    placed = (
        P("item", "tensor"),
        P("item", "tensor"),
        P("tensor", None),
        P(None, "tensor"),
        P(None, "tensor"),
        P("tensor"),
        P(None, "tensor"),
        P("item", None),
        P(None, None, "tensor"),
        P(None, None, "tensor"),
    )
    return jax.shard_map(
        functools.partial(shards, mesh.shape["item"]),
        mesh=mesh,
        in_specs=placed,
        out_specs=(P(None, None, "tensor"), P(None, None, "tensor")),
        check_vma=False,
    )
```

```python
import functools

import jax
import jax.numpy as jnp
from jax import lax
from jax.experimental import pallas as pl
from jax.experimental.pallas import tpu as pltpu
from jax.sharding import PartitionSpec as P

SCALE = 2.0
EPS = 1e-05
HI = lax.Precision.HIGHEST
F32 = jnp.float32
BF16 = jnp.bfloat16
N = 4
NT = (((1,), (1,)), ((), ()))
NN = (((1,), (0,)), ((), ()))


def dot(a, b, dims=NN, precision=None):
    return lax.dot_general(a, b, dims, preferred_element_type=F32, precision=precision)


def split3(v):
    a = v.astype(BF16)
    rest = v - a.astype(F32)
    b = rest.astype(BF16)
    c = (rest - b.astype(F32)).astype(BF16)
    return a, b, c


def wrap(v):
    return lax.rem(v, N)


def kernel(
    chunks, zs, total_tokens,
    x_hbm, r_hbm, w_hbm, a_ref, b_ref, g_ref, head_ref, prior_ref, v_ref, d_ref,
    out_ref,
    xt, xbuf, rbuf, wbuf, tb, r1, r2, pf, g8, avp, ybuf, gram, lbuf, la, lc, lx, lfull,
    hhi, hlo, ssend, sx, zpart, zrecv, zfull,
    wl, xl, rl, ws, wr, xs, xr, ms, mr, ns, nr, c1s, c1r, c2s, c2r, c3s, c3r, zss, zsr,
):
    piece, rows = x_hbm.shape
    half = rows // 2
    tc = half // chunks
    fb = r_hbm.shape[1]
    lanes = 128
    model = w_hbm.shape[1]
    rank = a_ref.shape[0]
    zi = lax.axis_index("item")
    me = lax.axis_index("tensor")
    core = lax.rem(me, 2)
    chip = lax.div(me, 2)
    px = lax.div(chip, N)
    py = lax.rem(chip, N)

    def device(x, y, c):
        return {"tensor": (x * N + y) * 2 + c}

    sibling = device(px, py, 1 - core)
    xpeer = [None] + [device(wrap(px + o), py, core) for o in range(1, N)]
    ypeer = [None] + [device(px, wrap(py + o), core) for o in range(1, N)]
    zpeer = [None] + [{"item": lax.rem(zi + o, zs)} for o in range(1, zs)]

    def far(i, j, c=0):
        return min(i, N - i) + min(j, N - j) + 0.1 * c

    plane = [(i, j, c) for i in range(N) for j in range(N) for c in range(2)][1:]
    plane.sort(key=lambda o: -far(*o))
    same = [o for o in plane if o[2] == 0]
    zorder = sorted(range(1, zs), key=lambda o: -min(o, zs - o))

    def away(o):
        return device(wrap(px + o[0]), wrap(py + o[1]), lax.rem(core + o[2], 2))

    sends = []

    def send(src, dst, ssem, rsem, to):
        copy = pltpu.make_async_remote_copy(
            src_ref=src, dst_ref=dst, send_sem=ssem, recv_sem=rsem,
            device_id=to, device_id_type=pl.DeviceIdType.MESH,
        )
        copy.start()
        sends.append(copy)
        return copy

    order = [(2, o) for o in range(N)] + [(o, 2) for o in (0, 1, 3)]
    order += [(i, j) for i in (1, 3, 0) for j in (1, 3, 0)]

    def block(n):
        return wrap(px + order[n][0]) * N + wrap(py + order[n][1])

    def columns(b, c):
        return pl.ds(pl.multiple_of((b * 2 + c) * fb, fb), fb)

    xloads = [
        pltpu.make_async_copy(x_hbm.at[:, pl.ds(f * half, half)], xt.at[0, :, pl.ds(f * half, half)], xl.at[f])
        for f in range(2)
    ]
    wloads = [
        pltpu.make_async_copy(w_hbm.at[:, columns(block(n), core)], wbuf.at[0, block(n)], wl.at[n])
        for n in range(N * N)
    ]
    rload = pltpu.make_async_copy(r_hbm, rbuf, rl.at[0])
    xloads[0].start()
    for n in range(N):
        wloads[n].start()
    xloads[1].start()
    for n in range(N, N * N):
        wloads[n].start()
    rload.start()

    g8[...] = jnp.zeros_like(g8)
    g8[0:4, :] = head_ref[...].astype(F32) * g_ref[...].astype(F32).reshape(1, fb)
    ghi = g8[...].astype(BF16).astype(F32)
    pf[:, :, 64:128, :] = jnp.zeros((N, N, 64, fb), BF16)
    pf[py, px, 0:rank, :] = b_ref[...]
    pf[py, px, rank:3 * rank, :] = d_ref[...]
    pf[py, px, 3 * rank:64, :] = jnp.concatenate([ghi, g8[...] - ghi], 0).astype(BF16)
    avp[...] = jnp.zeros_like(avp)
    avp[64:64 + rank, :] = a_ref[...]
    avp[64 + rank:64 + 3 * rank, :] = v_ref[...]

    barrier = pltpu.get_barrier_semaphore()
    peers = [away(o) for o in plane] + zpeer[1:]
    for to in peers:
        pl.semaphore_signal(barrier, inc=1, device_id=to, device_id_type=pl.DeviceIdType.MESH)
    pl.semaphore_wait(barrier, len(peers))

    def send_x(f):
        return send(x_hbm.at[:, pl.ds(f * half, half)], xt.at[1, :, pl.ds(f * half, half)], xs.at[f], xr.at[f], sibling)

    def send_w(n):
        return send(w_hbm.at[:, columns(block(n), 1 - core)], wbuf.at[1, block(n)], ws.at[n], wr.at[n], sibling)

    xin = [send_x(0)]
    win = [send_w(n) for n in range(N)]
    pin = [
        send(pf.at[py, px, pl.ds(0, 64)], pf.at[py, px, pl.ds(0, 64)], c1s.at[0, o - 1], c1r.at[0, o - 1], xpeer[o])
        for o in range(1, N)
    ]
    xin.append(send_x(1))
    win += [send_w(n) for n in range(N, N * N)]

    def recv_slot(src_shape_ref, sem):
        return pltpu.make_async_copy(src_shape_ref, src_shape_ref, sem)

    pos = [(px, py), (py, px)]

    eye = (
        lax.broadcasted_iota(jnp.int32, (lanes, lanes), 0) == lax.broadcasted_iota(jnp.int32, (lanes, lanes), 1)
    ).astype(F32).astype(BF16)

    def turn(s, f):
        for i in range(half // lanes):
            at = slice(f * half + i * lanes, f * half + (i + 1) * lanes)
            xbuf[s, at, :] = dot(eye, xt[s, :, at], NT).astype(BF16)

    def group(f, i1, lo=0, hi=N):
        def body(i2, carry):
            b = i1 * N + i2 if f == 0 else i2 * N + i1
            acc = dot(xbuf[0, f * half:(f + 1) * half, :], wbuf[0, b])
            acc = acc + dot(xbuf[1, f * half:(f + 1) * half, :], wbuf[1, b])
            out = acc.astype(BF16)
            tb[f, i1 * N + i2, 0] = out[:, :lanes]
            tb[f, i1 * N + i2, 1] = out[:, lanes:]
            return carry

        lax.fori_loop(lo, hi, body, 0)

    def send_m(f, c, direction, msg):
        peer = xpeer if f == 0 else ypeer
        to = peer[1] if direction == 0 else peer[N - 1]
        offset = 2 if msg == 0 else (1 if direction == 0 else N - 1)
        i1 = wrap(pos[f][0] + offset)
        part = 1 - direction if msg == 1 else direction
        send(
            tb.at[f, pl.ds(i1 * N + 2 * part, 2), :, pl.ds(c * tc, tc), :],
            r1.at[f, c, direction, msg],
            ms.at[f, c, direction, msg], mr.at[f, c, direction, msg], to,
        )

    def wait_m(f, c, direction, msg):
        recv_slot(r1.at[f, c, direction, msg], mr.at[f, c, direction, msg]).wait()

    def send_n(f, c, direction, msg):
        peer = ypeer if f == 0 else xpeer
        to = peer[1] if direction == 0 else peer[N - 1]
        offset = 2 if msg == 0 else (1 if direction == 0 else N - 1)
        i2 = wrap(pos[f][1] + offset)
        part = 1 - direction if msg == 1 else direction
        send(
            tb.at[f, pos[f][0] * N + i2, part, pl.ds(c * tc, tc), :],
            r2.at[f, c, direction, msg],
            ns.at[f, c, direction, msg], nr.at[f, c, direction, msg], to,
        )

    def wait_n(f, c, direction, msg):
        recv_slot(r2.at[f, c, direction, msg], nr.at[f, c, direction, msg]).wait()

    def wait_w(n):
        wloads[n].wait()
        win[n].wait_recv()

    def first(f):
        xloads[f].wait()
        turn(0, f)
        xin[f].wait_recv()
        turn(1, f)

    def start(f):
        for direction in range(2):
            group(f, wrap(pos[f][0] + 2), 2 * direction, 2 * direction + 2)
            for c in range(chunks):
                send_m(f, c, direction, 0)

    first(0)
    for n in range(N):
        wait_w(n)
    start(0)
    for copy in pin:
        copy.wait_recv()
    pin2 = [
        send(pf.at[py, :, pl.ds(0, 64)], pf.at[py, :, pl.ds(0, 64)], c1s.at[1, o - 1], c1r.at[1, o - 1], ypeer[o])
        for o in range(1, N)
    ]
    first(1)
    for n in range(N, 2 * N - 1):
        wait_w(n)
    start(1)
    for n in range(2 * N - 1, N * N):
        wait_w(n)

    def send_m2(f, c):
        for direction in range(2):
            send_m(f, c, direction, 1)

    for f in range(2):
        group(f, wrap(pos[f][0] + 1))
        group(f, wrap(pos[f][0] + N - 1))
        send_m2(f, 0)

    def middle(f, c):
        for direction in range(2):
            wait_m(f, c, direction, 0)
            i1 = wrap(pos[f][0] + (1 if direction == 0 else N - 1))
            at = (f, pl.ds(i1 * N + 2 * direction, 2), slice(None), pl.ds(c * tc, tc), slice(None))
            tb[at] = (tb[at].astype(F32) + r1[f, c, direction, 0].astype(F32)).astype(BF16)
            send_m(f, c, direction, 2)

    for f in range(2):
        middle(f, 0)
        send_m2(f, 1)
    group(0, pos[0][0])
    for f in range(2):
        middle(f, 1)
        send_m2(f, 2)
    group(1, pos[1][0])

    for copy in pin2:
        copy.wait_recv()
    for i in range(piece // 64):
        at = slice(i * 64, (i + 1) * 64)
        ybuf[0, at, :] = dot(eye[0:64, 0:64], avp[:, at], NT)
    ybuf[1] = jnp.zeros((piece, lanes), F32)
    gram[0] = jnp.zeros((64, lanes), F32)

    def project(b, carry):
        i, j = lax.div(b, N), lax.rem(b, N)
        p = pf[j, i]
        ybuf[0] = ybuf[0] + dot(wbuf[0, b], p, NT)
        ybuf[1] = ybuf[1] + dot(wbuf[1, b], p, NT)
        gram[0] = gram[0] + dot(p[0:64], p, NT)
        return carry

    lax.fori_loop(0, N * N // 2, project, 0)
    for f in range(2):
        middle(f, 2)
    lax.fori_loop(N * N // 2, N * N, project, 0)
    rload.wait()
    for s in range(2):
        for i, part in enumerate(split3(ybuf[s])):
            yi = part
            for f in range(2):
                at = slice(f * half, (f + 1) * half)
                add = dot(xbuf[s, at, :], yi)
                if s == 0 and i == 0:
                    lbuf[at, :] = dot(rbuf[at, :], pf[py, px], NT) + add
                else:
                    lbuf[at, :] = lbuf[at, :] + add
    other = pl.multiple_of((1 - core) * half, half)
    mine = pl.multiple_of(core * half, half)
    lin = send(lbuf.at[pl.ds(other, half)], la, c2s.at[0], c2r.at[0], sibling)
    gin = send(gram.at[0], gram.at[1], c2s.at[1], c2r.at[1], sibling)

    def stage2(f, c):
        wait_m(f, c, 0, 1)
        wait_m(f, c, 1, 1)
        wait_m(f, c, 0, 2)
        wait_m(f, c, 1, 2)
        for part in range(2):
            at = (f, pl.ds(pos[f][0] * N + 2 * part, 2), slice(None), pl.ds(c * tc, tc), slice(None))
            tb[at] = (
                tb[at].astype(F32)
                + r1[f, c, part, 2].astype(F32)
                + r1[f, c, 1 - part, 1].astype(F32)
            ).astype(BF16)
        for msg in range(2):
            for direction in range(2):
                send_n(f, c, direction, msg)

    def stage3(f, c):
        for direction in range(2):
            wait_n(f, c, direction, 0)
            i2 = wrap(pos[f][1] + (1 if direction == 0 else N - 1))
            at = (f, pos[f][0] * N + i2, direction, pl.ds(c * tc, tc), slice(None))
            tb[at] = (tb[at].astype(F32) + r2[f, c, direction, 0].astype(F32)).astype(BF16)
            send_n(f, c, direction, 2)

    for f in range(2):
        stage2(f, 0)
    lin.wait_recv()
    lc[...] = lbuf[pl.ds(mine, half), :] + la[...]
    q = half // (N * N)

    def part_of(o):
        return pl.ds(pl.multiple_of((wrap(px + o[0]) * N + wrap(py + o[1])) * q, q), q)

    bins = [send(lc.at[part_of(o)], lx.at[i], c2s.at[2 + i], c2r.at[2 + i], away(o)) for i, o in enumerate(same)]
    for f in range(2):
        stage2(f, 1)
    for f in range(2):
        stage3(f, 0)
    total = lc[part_of((0, 0)), :]
    for i, copy in enumerate(bins):
        copy.wait_recv()
        total = total + lx[i]
    lfull[core, px, py] = total
    own = lfull.at[core, px, py]
    dins = [send(own, own, c2s.at[17 + i], c2r.at[17 + i], away(o)) for i, o in enumerate(same)]
    for f in range(2):
        stage2(f, 2)
    for f in range(2):
        stage3(f, 1)
    for copy in dins:
        copy.wait_recv()
    own = lfull.at[core]
    fin = send(own, own, c2s.at[32], c2r.at[32], sibling)
    for f in range(2):
        stage3(f, 2)
    fin.wait_recv()
    gin.wait_recv()

    low = lfull[...].reshape(rows, lanes)
    lt = low.T
    gm = (gram[0] + gram[1])[:, 0:64]
    xa = lt[64:64 + rank]
    xv = [lt[64 + rank * (i + 1):64 + rank * (i + 2)] for i in range(2)]
    zero16 = jnp.zeros((rank, rows), F32)
    hp = lt[0:64] + SCALE * dot(gm, jnp.concatenate([xa, zero16, zero16, zero16], 0), precision=HI)
    hb = hp[0:rank]
    hg = hp[48:56] + hp[56:64]
    gm8 = gm[48:56] + gm[56:64]
    stacks = [
        jnp.concatenate([xv[0], xa, zero16, zero16], 0),
        jnp.concatenate([xv[1], zero16, xa, zero16], 0),
    ]
    dhg = [SCALE * dot(gm8, st, precision=HI) for st in stacks]
    mk = [
        SCALE / model * jnp.sum(xv[i] * hb + xa * hp[rank * (i + 1):rank * (i + 2)], 0, keepdims=True)
        for i in range(2)
    ]
    prior = jnp.concatenate([prior_ref[...], jnp.zeros((4, rows), F32)], 0)

    xa_cols = [part for part in split3(low)]
    shift = (
        lax.broadcasted_iota(jnp.int32, (lanes, rank), 0) == lax.broadcasted_iota(jnp.int32, (lanes, rank), 1) + 64
    ).astype(F32).astype(BF16)
    spread = dot(shift, b_ref[...]).astype(BF16)
    ssend[...] = jnp.zeros_like(ssend)
    for c in range(chunks):
        for f in range(2):
            for direction in range(2):
                wait_n(f, c, direction, 1)
                wait_n(f, c, direction, 2)
            at = slice(f * half + c * tc, f * half + (c + 1) * tc)
            ad = dot(xa_cols[0][at], spread) + dot(xa_cols[1][at], spread) + dot(xa_cols[2][at], spread)
            parts = []
            for part in range(2):
                parts.append(
                    tb[f, pos[f][0] * N + pos[f][1], part, c * tc:(c + 1) * tc, :].astype(F32)
                    + r2[f, c, part, 2].astype(F32)
                    + r2[f, c, 1 - part, 1].astype(F32)
                )
            h = jnp.concatenate(parts, 1) + rbuf[at, :].astype(F32) + SCALE * ad
            hi = h.astype(BF16)
            hhi[at, :] = hi
            hlo[at, :] = (h - hi.astype(F32)).astype(BF16)
            sq = h * h
            sq = sq[:, :lanes] + sq[:, lanes:]
            n = f * chunks + c
            ssend[n:n + 1, :] = jnp.sum(sq.T, 0, keepdims=True)

    ins = [send(ssend, sx.at[i], c3s.at[i], c3r.at[i], away(o)) for i, o in enumerate(plane)]
    stot = ssend[...]
    for i, copy in enumerate(ins):
        copy.wait_recv()
        stot = stot + sx[i]
    square = jnp.concatenate([stot[i:i + 1, :] for i in range(2 * chunks)], 1)

    r = lax.rsqrt(square / model + EPS)
    r3 = r * r * r
    live = lax.broadcasted_iota(jnp.int32, (8, rows), 0) < 4
    logits = jnp.where(live, r * hg + prior, -1e30)
    ex = jnp.where(live, jnp.exp(logits - jnp.max(logits, 0, keepdims=True)), 0.0)
    p = ex / jnp.sum(ex, 0, keepdims=True)
    us, cs, t1 = [], [], []
    gcol = gm[0:rank]
    for i in range(2):
        dl = r * dhg[i] - r3 * mk[i] * hg
        q = p * (dl - jnp.sum(p * dl, 0, keepdims=True)) / total_tokens
        s = jnp.sum(q * hg, 0, keepdims=True) / model
        back = dot(gcol, jnp.concatenate([zero16, zero16, zero16, q, q], 0), precision=HI)
        us.append(SCALE * (r * back - r3 * s * hb))
        cs.append(r3 * s * xa)
        t1.append(dot(xa, r * q, NT, precision=HI))
    uu = jnp.concatenate(split3(jnp.concatenate(us, 0)), 0)
    cc = jnp.concatenate(split3(jnp.concatenate(cs, 0)), 0)
    n32 = 2 * rank

    def fold(m):
        return m[0:n32] + m[n32:2 * n32] + m[2 * n32:3 * n32]

    ggn = fold(dot(uu, xbuf[0]))
    ch = fold(dot(cc, hhi[...]) + dot(cc, hlo[...]))
    curv = SCALE * (dot(jnp.concatenate(t1, 0), g8[...], precision=HI) - ch)

    zw = 3 * lanes
    for i in range(4):
        at = slice(8 * i, 8 * i + 8)
        zpart[2 * i] = ggn[at, 0:zw]
        zpart[2 * i + 1, :, 0:piece - zw] = ggn[at, zw:piece]
        zpart[2 * i + 1, :, lanes:zw] = curv[at, :]
    ins = []
    for o in zorder:
        ins.append(send(zpart.at[lax.rem(zi + o, zs)], zrecv.at[o - 1], zss.at[0, o - 1], zsr.at[0, o - 1], zpeer[o]))
    for copy in ins:
        copy.wait_recv()
    total = zpart[zi]
    for o in range(1, zs):
        total = total + zrecv[o - 1]
    zfull[zi] = total
    ins = [
        send(zfull.at[zi], zfull.at[zi], zss.at[1, o - 1], zsr.at[1, o - 1], zpeer[o]) for o in zorder
    ]
    for copy in ins:
        copy.wait_recv()
    out_ref[...] = zfull[...]
    for copy in sends:
        copy.wait_send()


def unpack(in_ref, ggn_ref, curv_ref):
    zw = in_ref.shape[2]
    piece = ggn_ref.shape[1]
    for i in range(4):
        at = slice(8 * i, 8 * i + 8)
        ggn_ref[at, 0:zw] = in_ref[2 * i]
        ggn_ref[at, zw:piece] = in_ref[2 * i + 1, :, 0:piece - zw]
        curv_ref[at, :] = in_ref[2 * i + 1, :, 128:zw]


def shards(zs, x, res, w, a_in, b_out, gain, head, prior, v_in, d_out):
    rows, piece = x.shape
    fb = res.shape[1]
    rank = a_in.shape[0]
    k = v_in.shape[0]
    chunks = 3
    half = rows // 2
    tc = half // chunks
    q = half // N // N
    vmem = pl.BlockSpec(memory_space=pltpu.VMEM)
    hbm = pl.BlockSpec(memory_space=pl.ANY)
    dma = pltpu.SemaphoreType.DMA
    packed = pl.pallas_call(
        functools.partial(kernel, chunks, zs, rows * zs),
        out_shape=jax.ShapeDtypeStruct((8, 8, 384), F32),
        in_specs=[hbm, hbm, hbm] + [vmem] * 7,
        out_specs=vmem,
        scratch_shapes=[
            pltpu.VMEM((2, piece, rows), BF16),
            pltpu.VMEM((2, rows, piece), BF16),
            pltpu.VMEM((rows, fb), BF16),
            pltpu.VMEM((2, N * N, piece, fb), BF16),
            pltpu.VMEM((2, N * N, 2, half, 128), BF16),
            pltpu.VMEM((2, chunks, 2, 3, 2, 2, tc, 128), BF16),
            pltpu.VMEM((2, chunks, 2, 3, tc, 128), BF16),
            pltpu.VMEM((N, N, 128, fb), BF16),
            pltpu.VMEM((8, fb), F32),
            pltpu.VMEM((128, piece), BF16),
            pltpu.VMEM((2, piece, 128), F32),
            pltpu.VMEM((2, 64, 128), F32),
            pltpu.VMEM((rows, 128), F32),
            pltpu.VMEM((half, 128), F32),
            pltpu.VMEM((half, 128), F32),
            pltpu.VMEM((N * N - 1, q, 128), F32),
            pltpu.VMEM((2, N, N, q, 128), F32),
            pltpu.VMEM((rows, fb), BF16),
            pltpu.VMEM((rows, fb), BF16),
            pltpu.VMEM((8, 128), F32),
            pltpu.VMEM((2 * N * N - 1, 8, 128), F32),
            pltpu.VMEM((8, 8, 384), F32),
            pltpu.VMEM((zs - 1, 8, 384), F32),
            pltpu.VMEM((8, 8, 384), F32),
            dma((N * N,)), dma((2,)), dma((1,)),
            dma((N * N,)), dma((N * N,)), dma((2,)), dma((2,)),
            dma((2, chunks, 2, 3)), dma((2, chunks, 2, 3)),
            dma((2, chunks, 2, 3)), dma((2, chunks, 2, 3)),
            dma((2, N - 1)), dma((2, N - 1)),
            dma((33,)), dma((33,)), dma((2 * N * N - 1,)), dma((2 * N * N - 1,)),
            dma((2, zs - 1)), dma((2, zs - 1)),
        ],
        compiler_params=pltpu.CompilerParams(
            collective_id=0, has_side_effects=True, vmem_limit_bytes=56 * 1024 * 1024
        ),
    )(
        x.T, res, w, a_in, b_out, gain, head, prior.T,
        v_in.reshape(k * rank, piece), d_out.reshape(k * rank, fb),
    )
    ggn, curv = pl.pallas_call(
        unpack,
        out_shape=(
            jax.ShapeDtypeStruct((k * rank, piece), F32),
            jax.ShapeDtypeStruct((k * rank, fb), F32),
        ),
    )(packed)
    return ggn.reshape(k, rank, piece), curv.reshape(k, rank, fb)


def solution(mesh):
    placed = (
        P("item", "tensor"),
        P("item", "tensor"),
        P("tensor", None),
        P(None, "tensor"),
        P(None, "tensor"),
        P("tensor"),
        P(None, "tensor"),
        P("item", None),
        P(None, None, "tensor"),
        P(None, None, "tensor"),
    )
    return jax.shard_map(
        functools.partial(shards, mesh.shape["item"]),
        mesh=mesh,
        in_specs=placed,
        out_specs=(P(None, None, "tensor"), P(None, None, "tensor")),
        check_vma=False,
    )
```

```python
import functools

import jax
import jax.numpy as jnp
from jax import lax
from jax.experimental import pallas as pl
from jax.experimental.pallas import tpu as pltpu
from jax.sharding import PartitionSpec as P

SCALE = 2.0
EPS = 1e-05
HI = lax.Precision.HIGHEST
F32 = jnp.float32
BF16 = jnp.bfloat16
N = 4
NT = (((1,), (1,)), ((), ()))
NN = (((1,), (0,)), ((), ()))


def dot(a, b, dims=NN, precision=None):
    return lax.dot_general(a, b, dims, preferred_element_type=F32, precision=precision)


def split3(v):
    a = v.astype(BF16)
    rest = v - a.astype(F32)
    b = rest.astype(BF16)
    c = (rest - b.astype(F32)).astype(BF16)
    return a, b, c


def wrap(v):
    return lax.rem(v, N)


def kernel(
    chunks, zs, total_tokens,
    x_hbm, r_hbm, w_hbm, a_hbm, b_hbm, g_hbm, head_hbm, prior_hbm, v_hbm, d_hbm,
    out_ref,
    a_ref, b_ref, g_ref, head_ref, prior_ref, v_ref, d_ref, sl,
    xt, xbuf, rbuf, wbuf, tb, r1, r2, pf, pown, g8, avp, ybuf, yin, gram, lbuf, la, lc, lx, lfull,
    hhi, hlo, ssend, sx, zpart, zrecv, zfull,
    wl, xl, rl, ws, wr, xs, xr, ms, mr, ns, nr, c1s, c1r, c2s, c2r, c3s, c3r, zss, zsr,
):
    piece, rows = x_hbm.shape
    half = rows // 2
    tc = half // chunks
    fb = r_hbm.shape[1]
    lanes = 128
    model = w_hbm.shape[1]
    rank = a_hbm.shape[0]
    zi = lax.axis_index("item")
    me = lax.axis_index("tensor")
    core = lax.rem(me, 2)
    chip = lax.div(me, 2)
    px = lax.div(chip, N)
    py = lax.rem(chip, N)

    def device(x, y, c):
        return {"tensor": (x * N + y) * 2 + c}

    sibling = device(px, py, 1 - core)
    xpeer = [None] + [device(wrap(px + o), py, core) for o in range(1, N)]
    ypeer = [None] + [device(px, wrap(py + o), core) for o in range(1, N)]
    zpeer = [None] + [{"item": lax.rem(zi + o, zs)} for o in range(1, zs)]

    def far(i, j, c=0):
        return min(i, N - i) + min(j, N - j) + 0.1 * c

    plane = [(i, j, c) for i in range(N) for j in range(N) for c in range(2)][1:]
    plane.sort(key=lambda o: -far(*o))
    same = [o for o in plane if o[2] == 0]
    zorder = sorted(range(1, zs), key=lambda o: -min(o, zs - o))

    def away(o):
        return device(wrap(px + o[0]), wrap(py + o[1]), lax.rem(core + o[2], 2))

    sends = []

    def send(src, dst, ssem, rsem, to):
        copy = pltpu.make_async_remote_copy(
            src_ref=src, dst_ref=dst, send_sem=ssem, recv_sem=rsem,
            device_id=to, device_id_type=pl.DeviceIdType.MESH,
        )
        copy.start()
        sends.append(copy)
        return copy

    barrier = pltpu.get_barrier_semaphore()
    peers = [away(o) for o in plane] + zpeer[1:]
    for to in peers:
        pl.semaphore_signal(barrier, inc=1, device_id=to, device_id_type=pl.DeviceIdType.MESH)

    order = [(2, o) for o in range(N)] + [(o, 2) for o in (0, 1, 3)]
    order += [(i, j) for i in (1, 3, 0) for j in (1, 3, 0)]

    def block(n):
        return wrap(px + order[n][0]) * N + wrap(py + order[n][1])

    def columns(b, c):
        return pl.ds(pl.multiple_of((b * 2 + c) * fb, fb), fb)

    xloads = [
        pltpu.make_async_copy(x_hbm.at[:, pl.ds(f * half, half)], xt.at[pl.ds(0, piece), pl.ds(f * half, half)], xl.at[f])
        for f in range(2)
    ]
    wloads = [
        pltpu.make_async_copy(w_hbm.at[:, columns(block(n), core)], wbuf.at[block(n), pl.ds(0, piece)], wl.at[n])
        for n in range(N * N)
    ]
    small = [
        pltpu.make_async_copy(src, dst, sl.at[i])
        for i, (src, dst) in enumerate([
            (b_hbm, b_ref), (d_hbm, d_ref), (g_hbm, g_ref), (head_hbm, head_ref), (a_hbm, a_ref), (v_hbm, v_ref),
            (prior_hbm, prior_ref),
        ])
    ]
    rload = pltpu.make_async_copy(r_hbm, rbuf, rl.at[0])
    for copy in small:
        copy.start()
    xloads[0].start()
    for n in range(N):
        wloads[n].start()
    xloads[1].start()
    for n in range(N, N * N):
        wloads[n].start()
    rload.start()
    for copy in small:
        copy.wait()

    g8[...] = jnp.zeros_like(g8)
    g8[0:4, :] = head_ref[...].astype(F32) * g_ref[...].astype(F32).reshape(1, fb)
    ghi = g8[...].astype(BF16).astype(F32)
    pf[:, :, 64:128, :] = jnp.zeros((N, N, 64, fb), BF16)
    pown[64:128, :] = jnp.zeros((64, fb), BF16)
    pown[0:rank, :] = b_ref[...]
    pown[rank:3 * rank, :] = d_ref[...]
    pown[3 * rank:64, :] = jnp.concatenate([ghi, g8[...] - ghi], 0).astype(BF16)
    avp[...] = jnp.zeros_like(avp)
    avp[64:64 + rank, :] = a_ref[...]
    avp[64 + rank:64 + 3 * rank, :] = v_ref[...]

    pf[py, px, 0:64, :] = pown[0:64, :]
    pl.semaphore_wait(barrier, len(peers))

    def send_x(f):
        return send(x_hbm.at[:, pl.ds(f * half, half)], xt.at[pl.ds(piece, piece), pl.ds(f * half, half)], xs.at[f], xr.at[f], sibling)

    def send_w(n):
        return send(w_hbm.at[:, columns(block(n), 1 - core)], wbuf.at[block(n), pl.ds(piece, piece)], ws.at[n], wr.at[n], sibling)

    xin = [send_x(0)]
    win = [send_w(n) for n in range(N)]
    pin = [
        send(pown.at[pl.ds(0, 64)], pf.at[py, px, pl.ds(0, 64)], c1s.at[i], c1r.at[i], away(o)) for i, o in enumerate(same)
    ]
    xin.append(send_x(1))
    win += [send_w(n) for n in range(N, N * N)]

    def recv_slot(src_shape_ref, sem):
        return pltpu.make_async_copy(src_shape_ref, src_shape_ref, sem)

    pos = [(px, py), (py, px)]

    eye = (
        lax.broadcasted_iota(jnp.int32, (lanes, lanes), 0) == lax.broadcasted_iota(jnp.int32, (lanes, lanes), 1)
    ).astype(F32).astype(BF16)

    def turn(f):
        for i in range(half // lanes):
            at = slice(f * half + i * lanes, f * half + (i + 1) * lanes)
            xbuf[at, :] = dot(eye, xt[:, at], NT).astype(BF16)

    def put(f, i1, i2, out):
        tb[f, i1 * N + i2, 0] = out[:, :lanes]
        tb[f, i1 * N + i2, 1] = out[:, lanes:]

    def group(f, i1, lo=0, hi=N):
        def body(i2, carry):
            b = i1 * N + i2 if f == 0 else i2 * N + i1
            put(f, i1, i2, dot(xbuf[f * half:(f + 1) * half, :], wbuf[b]).astype(BF16))
            return carry

        lax.fori_loop(lo, hi, body, 0)

    def both(count, ox, oy):
        def body(n, carry):
            x, y = wrap(px + ox(n)), wrap(py + oy(n))
            out = dot(xbuf[...], wbuf[x * N + y]).astype(BF16)
            put(0, x, y, out[:half])
            put(1, y, x, out[half:])
            return carry

        lax.fori_loop(0, count, body, 0)

    def single(f, offsets):
        def body(n, carry):
            i1, i2 = wrap(pos[f][0] + offsets(n)), wrap(pos[f][1] + 2)
            b = i1 * N + i2 if f == 0 else i2 * N + i1
            put(f, i1, i2, dot(xbuf[f * half:(f + 1) * half, :], wbuf[b]).astype(BF16))
            return carry

        return body

    def send_m(f, c, direction, msg):
        peer = xpeer if f == 0 else ypeer
        to = peer[1] if direction == 0 else peer[N - 1]
        offset = 2 if msg == 0 else (1 if direction == 0 else N - 1)
        i1 = wrap(pos[f][0] + offset)
        part = 1 - direction if msg == 1 else direction
        send(
            tb.at[f, pl.ds(i1 * N + 2 * part, 2), :, pl.ds(c * tc, tc), :],
            r1.at[f, c, direction, msg],
            ms.at[f, c, direction, msg], mr.at[f, c, direction, msg], to,
        )

    def wait_m(f, c, direction, msg):
        recv_slot(r1.at[f, c, direction, msg], mr.at[f, c, direction, msg]).wait()

    def send_n(f, c, direction, msg):
        peer = ypeer if f == 0 else xpeer
        to = peer[1] if direction == 0 else peer[N - 1]
        offset = 2 if msg == 0 else (1 if direction == 0 else N - 1)
        i2 = wrap(pos[f][1] + offset)
        part = 1 - direction if msg == 1 else direction
        send(
            tb.at[f, pos[f][0] * N + i2, part, pl.ds(c * tc, tc), :],
            r2.at[f, c, direction, msg],
            ns.at[f, c, direction, msg], nr.at[f, c, direction, msg], to,
        )

    def wait_n(f, c, direction, msg):
        recv_slot(r2.at[f, c, direction, msg], nr.at[f, c, direction, msg]).wait()

    def wait_w(n):
        wloads[n].wait()
        win[n].wait_recv()

    def first(f):
        xloads[f].wait()
        xin[f].wait_recv()
        turn(f)

    def start(f):
        for direction in range(2):
            group(f, wrap(pos[f][0] + 2), 2 * direction, 2 * direction + 2)
            for c in range(chunks):
                send_m(f, c, direction, 0)

    first(0)
    for n in range(N):
        wait_w(n)
    start(0)
    first(1)
    for n in range(N, 2 * N - 1):
        wait_w(n)
    start(1)
    for n in range(2 * N - 1, N * N):
        wait_w(n)

    def send_m2(f, c):
        for direction in range(2):
            send_m(f, c, direction, 1)

    both(4, lambda n: 1 + 2 * lax.div(n, 2), lambda n: 1 + 2 * lax.rem(n, 2))
    both(2, lambda n: 1 + 2 * n, lambda n: 0)
    lax.fori_loop(0, 2, single(0, lambda n: 1 + 2 * n), 0)
    send_m2(0, 0)
    both(2, lambda n: 0, lambda n: 1 + 2 * n)
    lax.fori_loop(0, 2, single(1, lambda n: 1 + 2 * n), 0)
    send_m2(1, 0)

    def middle(f, c):
        for direction in range(2):
            wait_m(f, c, direction, 0)
            i1 = wrap(pos[f][0] + (1 if direction == 0 else N - 1))
            at = (f, pl.ds(i1 * N + 2 * direction, 2), slice(None), pl.ds(c * tc, tc), slice(None))
            tb[at] = (tb[at].astype(F32) + r1[f, c, direction, 0].astype(F32)).astype(BF16)
            send_m(f, c, direction, 2)

    for f in range(2):
        middle(f, 0)
        send_m2(f, 1)
    both(1, lambda n: n, lambda n: n)
    for f in range(2):
        lax.fori_loop(0, 1, single(f, lambda n: n), 0)
    for f in range(2):
        middle(f, 1)
        send_m2(f, 2)
    for f in range(2):
        middle(f, 2)

    for copy in pin:
        copy.wait_recv()
    for i in range(piece // 64):
        at = slice(i * 64, (i + 1) * 64)
        ybuf[at, :] = dot(eye[0:64, 0:64], avp[:, at], NT)
    ybuf[piece:, :] = jnp.zeros((piece, lanes), F32)
    gram[0] = jnp.zeros((64, lanes), F32)

    def project(j, carry):
        acc, g = 0.0, 0.0
        for i in range(N):
            p = pf[j, i]
            acc = acc + dot(wbuf[i * N + j], p, NT)
            g = g + dot(p[0:64], p, NT)
        ybuf[...] = ybuf[...] + acc
        gram[0] = gram[0] + g
        return carry

    lax.fori_loop(0, N, project, 0)
    yx = [
        send(ybuf.at[pl.ds(s * piece, piece)], yin.at[pl.ds((1 - s) * piece, piece)], c2s.at[33 + s], c2r.at[33 + s], sibling)
        for s in range(2)
    ]
    gin = send(gram.at[0], gram.at[1], c2s.at[1], c2r.at[1], sibling)
    other = pl.multiple_of((1 - core) * half, half)
    mine = pl.multiple_of(core * half, half)
    rload.wait()
    lbuf[...] = dot(rbuf[...], pown[...], NT)
    lin = send(lbuf.at[pl.ds(other, half)], la, c2s.at[0], c2r.at[0], sibling)

    def stage2(f, c):
        wait_m(f, c, 0, 1)
        wait_m(f, c, 1, 1)
        wait_m(f, c, 0, 2)
        wait_m(f, c, 1, 2)
        for part in range(2):
            at = (f, pl.ds(pos[f][0] * N + 2 * part, 2), slice(None), pl.ds(c * tc, tc), slice(None))
            tb[at] = (
                tb[at].astype(F32)
                + r1[f, c, part, 2].astype(F32)
                + r1[f, c, 1 - part, 1].astype(F32)
            ).astype(BF16)
        for msg in range(2):
            for direction in range(2):
                send_n(f, c, direction, msg)

    def stage3(f, c):
        for direction in range(2):
            wait_n(f, c, direction, 0)
            i2 = wrap(pos[f][1] + (1 if direction == 0 else N - 1))
            at = (f, pos[f][0] * N + i2, direction, pl.ds(c * tc, tc), slice(None))
            tb[at] = (tb[at].astype(F32) + r2[f, c, direction, 0].astype(F32)).astype(BF16)
            send_n(f, c, direction, 2)

    for copy in yx:
        copy.wait_recv()
    lin.wait_recv()
    total = lbuf[pl.ds(mine, half), :] + la[...]
    for part in split3(ybuf[...] + yin[...]):
        total = total + dot(xbuf[pl.ds(mine, half), :], part)
    lc[...] = total
    q = half // (N * N)

    def part_of(o):
        return pl.ds(pl.multiple_of((wrap(px + o[0]) * N + wrap(py + o[1])) * q, q), q)

    bins = [send(lc.at[part_of(o)], lx.at[i], c2s.at[2 + i], c2r.at[2 + i], away(o)) for i, o in enumerate(same)]
    stage2(0, 0)
    stage2(1, 0)
    stage2(0, 1)
    stage3(0, 0)
    stage2(1, 1)
    stage3(1, 0)
    total = lc[part_of((0, 0)), :]
    for i, copy in enumerate(bins):
        copy.wait_recv()
        total = total + lx[i]
    lfull[core, px, py] = total
    own = lfull.at[core, px, py]
    dins = [send(own, own, c2s.at[17 + i], c2r.at[17 + i], away(o)) for i, o in enumerate(same)]
    stage2(0, 2)
    stage3(0, 1)
    stage2(1, 2)
    stage3(1, 1)
    for copy in dins:
        copy.wait_recv()
    own = lfull.at[core]
    fin = send(own, own, c2s.at[32], c2r.at[32], sibling)
    for f in range(2):
        stage3(f, 2)
    fin.wait_recv()
    gin.wait_recv()

    low = lfull[...].reshape(rows, lanes)
    lt = low.T
    gm = (gram[0] + gram[1])[:, 0:64]
    xa = lt[64:64 + rank]
    xv = [lt[64 + rank * (i + 1):64 + rank * (i + 2)] for i in range(2)]
    zero16 = jnp.zeros((rank, rows), F32)
    hp = lt[0:64] + SCALE * dot(gm, jnp.concatenate([xa, zero16, zero16, zero16], 0), precision=HI)
    hb = hp[0:rank]
    hg = hp[48:56] + hp[56:64]
    gm8 = gm[48:56] + gm[56:64]
    stacks = [
        jnp.concatenate([xv[0], xa, zero16, zero16], 0),
        jnp.concatenate([xv[1], zero16, xa, zero16], 0),
    ]
    dhg = [SCALE * dot(gm8, st, precision=HI) for st in stacks]
    mk = [
        SCALE / model * jnp.sum(xv[i] * hb + xa * hp[rank * (i + 1):rank * (i + 2)], 0, keepdims=True)
        for i in range(2)
    ]
    prior = jnp.concatenate([prior_ref[...], jnp.zeros((4, rows), F32)], 0)

    xa_cols = [part for part in split3(low)]
    shift = (
        lax.broadcasted_iota(jnp.int32, (lanes, rank), 0) == lax.broadcasted_iota(jnp.int32, (lanes, rank), 1) + 64
    ).astype(F32).astype(BF16)
    spread = dot(shift, b_ref[...]).astype(BF16)
    ssend[...] = jnp.zeros_like(ssend)
    for c in range(chunks):
        for f in range(2):
            for direction in range(2):
                wait_n(f, c, direction, 1)
                wait_n(f, c, direction, 2)
            at = slice(f * half + c * tc, f * half + (c + 1) * tc)
            ad = dot(xa_cols[0][at], spread) + dot(xa_cols[1][at], spread) + dot(xa_cols[2][at], spread)
            parts = []
            for part in range(2):
                parts.append(
                    tb[f, pos[f][0] * N + pos[f][1], part, c * tc:(c + 1) * tc, :].astype(F32)
                    + r2[f, c, part, 2].astype(F32)
                    + r2[f, c, 1 - part, 1].astype(F32)
                )
            h = jnp.concatenate(parts, 1) + rbuf[at, :].astype(F32) + SCALE * ad
            hi = h.astype(BF16)
            hhi[at, :] = hi
            hlo[at, :] = (h - hi.astype(F32)).astype(BF16)
            sq = h * h
            sq = sq[:, :lanes] + sq[:, lanes:]
            n = f * chunks + c
            ssend[n:n + 1, :] = jnp.sum(sq.T, 0, keepdims=True)

    ins = [send(ssend, sx.at[i], c3s.at[i], c3r.at[i], away(o)) for i, o in enumerate(plane)]
    for copy in sends[:-len(ins)]:
        copy.wait_send()
    late = len(sends) - len(ins)
    stot = ssend[...]
    for i, copy in enumerate(ins):
        copy.wait_recv()
        stot = stot + sx[i]
    square = jnp.concatenate([stot[i:i + 1, :] for i in range(2 * chunks)], 1)

    r = lax.rsqrt(square / model + EPS)
    r3 = r * r * r
    live = lax.broadcasted_iota(jnp.int32, (8, rows), 0) < 4
    logits = jnp.where(live, r * hg + prior, -1e30)
    ex = jnp.where(live, jnp.exp(logits - jnp.max(logits, 0, keepdims=True)), 0.0)
    p = ex / jnp.sum(ex, 0, keepdims=True)
    us, cs, t1 = [], [], []
    gcol = gm[0:rank]
    for i in range(2):
        dl = r * dhg[i] - r3 * mk[i] * hg
        q = p * (dl - jnp.sum(p * dl, 0, keepdims=True)) / total_tokens
        s = jnp.sum(q * hg, 0, keepdims=True) / model
        back = dot(gcol, jnp.concatenate([zero16, zero16, zero16, q, q], 0), precision=HI)
        us.append(SCALE * (r * back - r3 * s * hb))
        cs.append(r3 * s * xa)
        t1.append(dot(xa, r * q, NT, precision=HI))
    uu = jnp.concatenate(split3(jnp.concatenate(us, 0)), 0)
    cc = jnp.concatenate(split3(jnp.concatenate(cs, 0)), 0)
    n32 = 2 * rank

    def fold(m):
        return m[0:n32] + m[n32:2 * n32] + m[2 * n32:3 * n32]

    ggn = fold(dot(uu, xbuf[:, 0:piece]))
    ch = fold(dot(cc, hhi[...]) + dot(cc, hlo[...]))
    curv = SCALE * (dot(jnp.concatenate(t1, 0), g8[...], precision=HI) - ch)

    zw = 3 * lanes
    for i in range(4):
        at = slice(8 * i, 8 * i + 8)
        zpart[2 * i] = ggn[at, 0:zw]
        zpart[2 * i + 1, :, 0:piece - zw] = ggn[at, zw:piece]
        zpart[2 * i + 1, :, lanes:zw] = curv[at, :]
    ins = []
    for o in zorder:
        ins.append(send(zpart.at[lax.rem(zi + o, zs)], zrecv.at[o - 1], zss.at[0, o - 1], zsr.at[0, o - 1], zpeer[o]))
    for copy in ins:
        copy.wait_recv()
    total = zpart[zi]
    for o in range(1, zs):
        total = total + zrecv[o - 1]
    zfull[zi] = total
    ins = [
        send(zfull.at[zi], zfull.at[zi], zss.at[1, o - 1], zsr.at[1, o - 1], zpeer[o]) for o in zorder
    ]
    for copy in ins:
        copy.wait_recv()
    out_ref[...] = zfull[...]
    for copy in sends[late:]:
        copy.wait_send()


def unpack(in_ref, ggn_ref, curv_ref):
    zw = in_ref.shape[2]
    piece = ggn_ref.shape[1]
    for i in range(4):
        at = slice(8 * i, 8 * i + 8)
        ggn_ref[at, 0:zw] = in_ref[2 * i]
        ggn_ref[at, zw:piece] = in_ref[2 * i + 1, :, 0:piece - zw]
        curv_ref[at, :] = in_ref[2 * i + 1, :, 128:zw]


def shards(zs, x, res, w, a_in, b_out, gain, head, prior, v_in, d_out):
    rows, piece = x.shape
    fb = res.shape[1]
    rank = a_in.shape[0]
    k = v_in.shape[0]
    chunks = 3
    half = rows // 2
    tc = half // chunks
    q = half // N // N
    vmem = pl.BlockSpec(memory_space=pltpu.VMEM)
    hbm = pl.BlockSpec(memory_space=pl.ANY)
    dma = pltpu.SemaphoreType.DMA
    packed = pl.pallas_call(
        functools.partial(kernel, chunks, zs, rows * zs),
        out_shape=jax.ShapeDtypeStruct((8, 8, 384), F32),
        in_specs=[hbm] * 10,
        out_specs=vmem,
        scratch_shapes=[
            pltpu.VMEM(a_in.shape, BF16),
            pltpu.VMEM(b_out.shape, BF16),
            pltpu.VMEM(gain.shape, BF16),
            pltpu.VMEM(head.shape, BF16),
            pltpu.VMEM((prior.shape[1], rows), F32),
            pltpu.VMEM((k * rank, piece), BF16),
            pltpu.VMEM((k * rank, fb), BF16),
            dma((7,)),
            pltpu.VMEM((2 * piece, rows), BF16),
            pltpu.VMEM((rows, 2 * piece), BF16),
            pltpu.VMEM((rows, fb), BF16),
            pltpu.VMEM((N * N, 2 * piece, fb), BF16),
            pltpu.VMEM((2, N * N, 2, half, 128), BF16),
            pltpu.VMEM((2, chunks, 2, 3, 2, 2, tc, 128), BF16),
            pltpu.VMEM((2, chunks, 2, 3, tc, 128), BF16),
            pltpu.VMEM((N, N, 128, fb), BF16),
            pltpu.VMEM((128, fb), BF16),
            pltpu.VMEM((8, fb), F32),
            pltpu.VMEM((128, piece), BF16),
            pltpu.VMEM((2 * piece, 128), F32),
            pltpu.VMEM((2 * piece, 128), F32),
            pltpu.VMEM((2, 64, 128), F32),
            pltpu.VMEM((rows, 128), F32),
            pltpu.VMEM((half, 128), F32),
            pltpu.VMEM((half, 128), F32),
            pltpu.VMEM((N * N - 1, q, 128), F32),
            pltpu.VMEM((2, N, N, q, 128), F32),
            pltpu.VMEM((rows, fb), BF16),
            pltpu.VMEM((rows, fb), BF16),
            pltpu.VMEM((8, 128), F32),
            pltpu.VMEM((2 * N * N - 1, 8, 128), F32),
            pltpu.VMEM((8, 8, 384), F32),
            pltpu.VMEM((zs - 1, 8, 384), F32),
            pltpu.VMEM((8, 8, 384), F32),
            dma((N * N,)), dma((2,)), dma((1,)),
            dma((N * N,)), dma((N * N,)), dma((2,)), dma((2,)),
            dma((2, chunks, 2, 3)), dma((2, chunks, 2, 3)),
            dma((2, chunks, 2, 3)), dma((2, chunks, 2, 3)),
            dma((N * N - 1,)), dma((N * N - 1,)),
            dma((35,)), dma((35,)), dma((2 * N * N - 1,)), dma((2 * N * N - 1,)),
            dma((2, zs - 1)), dma((2, zs - 1)),
        ],
        compiler_params=pltpu.CompilerParams(
            collective_id=0, has_side_effects=True, vmem_limit_bytes=56 * 1024 * 1024
        ),
    )(
        x.T, res, w, a_in, b_out, gain, head, prior.T,
        v_in.reshape(k * rank, piece), d_out.reshape(k * rank, fb),
    )
    ggn, curv = pl.pallas_call(
        unpack,
        out_shape=(
            jax.ShapeDtypeStruct((k * rank, piece), F32),
            jax.ShapeDtypeStruct((k * rank, fb), F32),
        ),
    )(packed)
    return ggn.reshape(k, rank, piece), curv.reshape(k, rank, fb)


def solution(mesh):
    placed = (
        P("item", "tensor"),
        P("item", "tensor"),
        P("tensor", None),
        P(None, "tensor"),
        P(None, "tensor"),
        P("tensor"),
        P(None, "tensor"),
        P("item", None),
        P(None, None, "tensor"),
        P(None, None, "tensor"),
    )
    return jax.shard_map(
        functools.partial(shards, mesh.shape["item"]),
        mesh=mesh,
        in_specs=placed,
        out_specs=(P(None, None, "tensor"), P(None, None, "tensor")),
        check_vma=False,
    )
```

```python
import functools

import jax
import jax.numpy as jnp
from jax import lax
from jax.experimental import pallas as pl
from jax.experimental.pallas import tpu as pltpu
from jax.sharding import PartitionSpec as P

SCALE = 2.0
EPS = 1e-05
HI = lax.Precision.HIGHEST
F32 = jnp.float32
BF16 = jnp.bfloat16
N = 4
NT = (((1,), (1,)), ((), ()))
NN = (((1,), (0,)), ((), ()))


def dot(a, b, dims=NN, precision=None):
    return lax.dot_general(a, b, dims, preferred_element_type=F32, precision=precision)


def split3(v):
    a = v.astype(BF16)
    rest = v - a.astype(F32)
    b = rest.astype(BF16)
    c = (rest - b.astype(F32)).astype(BF16)
    return a, b, c


def wrap(v):
    return lax.rem(v, N)


def kernel(
    chunks, zs, total_tokens,
    x_hbm, r_hbm, w_hbm, a_hbm, b_hbm, g_hbm, head_hbm, prior_hbm, v_hbm, d_hbm,
    out_ref,
    a_ref, b_ref, g_ref, head_ref, prior_ref, v_ref, d_ref, sl,
    xt, xbuf, rbuf, wbuf, tb, r1, r2, pf, pown, g8, avp, ybuf, yin, gram, lbuf, la, lc, lx, lfull,
    hhi, hlo, ssend, sx, zpart, zrecv, zfull,
    wl, xl, rl, ws, wr, xs, xr, ms, mr, ns, nr, c1s, c1r, c2s, c2r, c3s, c3r, zss, zsr, met,
):
    piece, rows = x_hbm.shape
    half = rows // 2
    tc = half // chunks
    fb = r_hbm.shape[1]
    lanes = 128
    model = w_hbm.shape[1]
    rank = a_hbm.shape[0]
    zi = lax.axis_index("item")
    me = lax.axis_index("tensor")
    core = lax.rem(me, 2)
    chip = lax.div(me, 2)
    px = lax.div(chip, N)
    py = lax.rem(chip, N)

    def device(x, y, c):
        return {"tensor": (x * N + y) * 2 + c}

    sibling = device(px, py, 1 - core)
    xpeer = [None] + [device(wrap(px + o), py, core) for o in range(1, N)]
    ypeer = [None] + [device(px, wrap(py + o), core) for o in range(1, N)]
    zpeer = [None] + [{"item": lax.rem(zi + o, zs)} for o in range(1, zs)]

    def far(i, j, c=0):
        return min(i, N - i) + min(j, N - j) + 0.1 * c

    plane = [(i, j, c) for i in range(N) for j in range(N) for c in range(2)][1:]
    plane.sort(key=lambda o: -far(*o))
    same = [o for o in plane if o[2] == 0]
    zorder = sorted(range(1, zs), key=lambda o: -min(o, zs - o))

    def away(o):
        return device(wrap(px + o[0]), wrap(py + o[1]), lax.rem(core + o[2], 2))

    sends = []

    def send(src, dst, ssem, rsem, to):
        copy = pltpu.make_async_remote_copy(
            src_ref=src, dst_ref=dst, send_sem=ssem, recv_sem=rsem,
            device_id=to, device_id_type=pl.DeviceIdType.MESH,
        )
        copy.start()
        sends.append(copy)
        return copy

    barrier = pltpu.get_barrier_semaphore()
    peers = [sibling] + xpeer[1:] + ypeer[1:] + [zpeer[1], zpeer[zs - 1]]
    for to in peers:
        pl.semaphore_signal(barrier, inc=1, device_id=to, device_id_type=pl.DeviceIdType.MESH)

    order = [(2, o) for o in range(N)] + [(o, 2) for o in (0, 1, 3)]
    order += [(i, j) for i in (1, 3, 0) for j in (3, 0, 1)]

    def block(n):
        return wrap(px + order[n][0]) * N + wrap(py + order[n][1])

    def columns(b, c):
        return pl.ds(pl.multiple_of((b * 2 + c) * fb, fb), fb)

    xloads = [
        pltpu.make_async_copy(x_hbm.at[:, pl.ds(f * half, half)], xt.at[pl.ds(0, piece), pl.ds(f * half, half)], xl.at[f])
        for f in range(2)
    ]
    wloads = [
        pltpu.make_async_copy(w_hbm.at[:, columns(block(n), core)], wbuf.at[block(n), pl.ds(0, piece)], wl.at[n])
        for n in range(N * N)
    ]
    small = [
        pltpu.make_async_copy(src, dst, sl.at[i])
        for i, (src, dst) in enumerate([
            (b_hbm, b_ref), (d_hbm, d_ref), (g_hbm, g_ref), (head_hbm, head_ref), (a_hbm, a_ref), (v_hbm, v_ref),
            (prior_hbm, prior_ref),
        ])
    ]
    rload = pltpu.make_async_copy(r_hbm, rbuf, rl.at[0])
    for copy in small:
        copy.start()
    xloads[0].start()
    for n in range(N):
        wloads[n].start()
    xloads[1].start()
    for n in range(N, N * N):
        wloads[n].start()
    rload.start()
    for copy in small:
        copy.wait()

    g8[...] = jnp.zeros_like(g8)
    g8[0:4, :] = head_ref[...].astype(F32) * g_ref[...].astype(F32).reshape(1, fb)
    ghi = g8[...].astype(BF16).astype(F32)
    pf[:, :, 64:128, :] = jnp.zeros((N, N, 64, fb), BF16)
    pown[64:128, :] = jnp.zeros((64, fb), BF16)
    pown[0:rank, :] = b_ref[...]
    pown[rank:3 * rank, :] = d_ref[...]
    pown[3 * rank:64, :] = jnp.concatenate([ghi, g8[...] - ghi], 0).astype(BF16)
    avp[...] = jnp.zeros_like(avp)
    avp[64:64 + rank, :] = a_ref[...]
    avp[64 + rank:64 + 3 * rank, :] = v_ref[...]

    share = pl.ds(pl.multiple_of(lax.rem(zi, 2) * 32, 32), 32)
    pf[py, px, share, :] = pown[share, :]
    pl.semaphore_wait(barrier, len(peers))

    def send_x(f):
        return send(x_hbm.at[:, pl.ds(f * half, half)], xt.at[pl.ds(piece, piece), pl.ds(f * half, half)], xs.at[f], xr.at[f], sibling)

    def send_w(n):
        return send(w_hbm.at[:, columns(block(n), 1 - core)], wbuf.at[block(n), pl.ds(piece, piece)], ws.at[n], wr.at[n], sibling)

    xin = [send_x(0)]
    win = [send_w(n) for n in range(N)]
    pin = [
        send(pown.at[share], pf.at[py, px, share], c1s.at[o - 1], c1r.at[o - 1], xpeer[o]) for o in (2, 1, 3)
    ]
    xin.append(send_x(1))
    win += [send_w(n) for n in range(N, N * N)]

    def recv_slot(src_shape_ref, sem):
        return pltpu.make_async_copy(src_shape_ref, src_shape_ref, sem)

    pos = [(px, py), (py, px)]

    eye = (
        lax.broadcasted_iota(jnp.int32, (lanes, lanes), 0) == lax.broadcasted_iota(jnp.int32, (lanes, lanes), 1)
    ).astype(F32).astype(BF16)

    def turn(f):
        for i in range(half // lanes):
            at = slice(f * half + i * lanes, f * half + (i + 1) * lanes)
            xbuf[at, :] = dot(eye, xt[:, at], NT).astype(BF16)

    def put(f, i1, i2, out):
        tb[f, i1 * N + i2, 0] = out[:, :lanes]
        tb[f, i1 * N + i2, 1] = out[:, lanes:]

    def group(f, i1, lo=0, hi=N):
        def body(i2, carry):
            b = i1 * N + i2 if f == 0 else i2 * N + i1
            put(f, i1, i2, dot(xbuf[f * half:(f + 1) * half, :], wbuf[b]).astype(BF16))
            return carry

        lax.fori_loop(lo, hi, body, 0)

    def both(count, ox, oy):
        def body(n, carry):
            x, y = wrap(px + ox(n)), wrap(py + oy(n))
            out = dot(xbuf[...], wbuf[x * N + y]).astype(BF16)
            put(0, x, y, out[:half])
            put(1, y, x, out[half:])
            return carry

        lax.fori_loop(0, count, body, 0)

    def single(f, offsets):
        def body(n, carry):
            i1, i2 = wrap(pos[f][0] + offsets(n)), wrap(pos[f][1] + 2)
            b = i1 * N + i2 if f == 0 else i2 * N + i1
            put(f, i1, i2, dot(xbuf[f * half:(f + 1) * half, :], wbuf[b]).astype(BF16))
            return carry

        return body

    def send_m(f, c, direction, msg):
        peer = xpeer if f == 0 else ypeer
        to = peer[1] if direction == 0 else peer[N - 1]
        offset = 2 if msg == 0 else (1 if direction == 0 else N - 1)
        i1 = wrap(pos[f][0] + offset)
        part = 1 - direction if msg == 1 else direction
        send(
            tb.at[f, pl.ds(i1 * N + 2 * part, 2), :, pl.ds(c * tc, tc), :],
            r1.at[f, c, direction, msg],
            ms.at[f, c, direction, msg], mr.at[f, c, direction, msg], to,
        )

    def wait_m(f, c, direction, msg):
        recv_slot(r1.at[f, c, direction, msg], mr.at[f, c, direction, msg]).wait()

    def send_n(f, c, direction, msg):
        peer = ypeer if f == 0 else xpeer
        to = peer[1] if direction == 0 else peer[N - 1]
        offset = 2 if msg == 0 else (1 if direction == 0 else N - 1)
        i2 = wrap(pos[f][1] + offset)
        part = 1 - direction if msg == 1 else direction
        send(
            tb.at[f, pos[f][0] * N + i2, part, pl.ds(c * tc, tc), :],
            r2.at[f, c, direction, msg],
            ns.at[f, c, direction, msg], nr.at[f, c, direction, msg], to,
        )

    def wait_n(f, c, direction, msg):
        recv_slot(r2.at[f, c, direction, msg], nr.at[f, c, direction, msg]).wait()

    def wait_w(n):
        wloads[n].wait()
        win[n].wait_recv()

    def first(f):
        xloads[f].wait()
        xin[f].wait_recv()
        turn(f)

    def start(f):
        for direction in range(2):
            group(f, wrap(pos[f][0] + 2), 2 * direction, 2 * direction + 2)
            for c in range(chunks):
                send_m(f, c, direction, 0)

    first(0)
    for n in range(N):
        wait_w(n)
    start(0)
    for copy in pin:
        copy.wait_recv()
    pin = [
        send(pf.at[py, :, share], pf.at[py, :, share], c1s.at[2 + o], c1r.at[2 + o], ypeer[o]) for o in (2, 1, 3)
    ]
    first(1)
    for n in range(N, 2 * N - 1):
        wait_w(n)
    start(1)

    def greet(n):
        for to in (zpeer[1], zpeer[zs - 1]):
            pl.semaphore_signal(met.at[n], inc=1, device_id=to, device_id_type=pl.DeviceIdType.MESH)

    greet(0)
    def send_m2(f, c):
        for direction in range(2):
            send_m(f, c, direction, 1)

    for i, o in enumerate((1, 3)):
        for n in range(2 * N - 1 + 3 * i, 2 * N + 2 + 3 * i):
            wait_w(n)
        both(3, lambda n: o, lambda n: N - 1 + n)
        lax.fori_loop(0, 1, single(0, lambda n: o + n), 0)
        send_m(0, 0, i, 1)
    for copy in pin:
        copy.wait_recv()
    pair = {"item": zi + 1 - 2 * lax.rem(zi, 2)}
    pin = [send(pf.at[:, :, share], pf.at[:, :, share], c1s.at[6], c1r.at[6], pair)]
    for n in range(N * N - 3, N * N):
        wait_w(n)
    for i, o in enumerate((1, 3)):
        both(1, lambda n: n, lambda n: o + n)
        lax.fori_loop(0, 1, single(1, lambda n: o + n), 0)
        send_m(1, 0, i, 1)

    def middle(f, c):
        for direction in range(2):
            wait_m(f, c, direction, 0)
            i1 = wrap(pos[f][0] + (1 if direction == 0 else N - 1))
            at = (f, pl.ds(i1 * N + 2 * direction, 2), slice(None), pl.ds(c * tc, tc), slice(None))
            tb[at] = (tb[at].astype(F32) + r1[f, c, direction, 0].astype(F32)).astype(BF16)
            send_m(f, c, direction, 2)

    for f in range(2):
        middle(f, 0)
        send_m2(f, 1)
    both(1, lambda n: n, lambda n: n)
    for f in range(2):
        lax.fori_loop(0, 1, single(f, lambda n: n), 0)
    for f in range(2):
        middle(f, 1)
        send_m2(f, 2)
    for f in range(2):
        middle(f, 2)

    pl.semaphore_wait(met.at[0], 2)
    greet(1)

    for copy in pin:
        copy.wait_recv()
    for i in range(piece // 64):
        at = slice(i * 64, (i + 1) * 64)
        ybuf[at, :] = dot(eye[0:64, 0:64], avp[:, at], NT)
    ybuf[piece:, :] = jnp.zeros((piece, lanes), F32)
    gram[0] = jnp.zeros((64, lanes), F32)

    def project(j, carry):
        acc, g = 0.0, 0.0
        for i in range(N):
            p = pf[j, i]
            acc = acc + dot(wbuf[i * N + j], p, NT)
            g = g + dot(p[0:64], p, NT)
        ybuf[...] = ybuf[...] + acc
        gram[0] = gram[0] + g
        return carry

    lax.fori_loop(0, N, project, 0)
    yx = [
        send(ybuf.at[pl.ds(s * piece, piece)], yin.at[pl.ds((1 - s) * piece, piece)], c2s.at[33 + s], c2r.at[33 + s], sibling)
        for s in range(2)
    ]
    gin = send(gram.at[0], gram.at[1], c2s.at[1], c2r.at[1], sibling)
    other = pl.multiple_of((1 - core) * half, half)
    mine = pl.multiple_of(core * half, half)
    rload.wait()
    lbuf[...] = dot(rbuf[...], pown[...], NT)
    lin = send(lbuf.at[pl.ds(other, half)], la, c2s.at[0], c2r.at[0], sibling)

    def stage2(f, c):
        wait_m(f, c, 0, 1)
        wait_m(f, c, 1, 1)
        wait_m(f, c, 0, 2)
        wait_m(f, c, 1, 2)
        for part in range(2):
            at = (f, pl.ds(pos[f][0] * N + 2 * part, 2), slice(None), pl.ds(c * tc, tc), slice(None))
            tb[at] = (
                tb[at].astype(F32)
                + r1[f, c, part, 2].astype(F32)
                + r1[f, c, 1 - part, 1].astype(F32)
            ).astype(BF16)
        for msg in range(2):
            for direction in range(2):
                send_n(f, c, direction, msg)

    def stage3(f, c):
        for direction in range(2):
            wait_n(f, c, direction, 0)
            i2 = wrap(pos[f][1] + (1 if direction == 0 else N - 1))
            at = (f, pos[f][0] * N + i2, direction, pl.ds(c * tc, tc), slice(None))
            tb[at] = (tb[at].astype(F32) + r2[f, c, direction, 0].astype(F32)).astype(BF16)
            send_n(f, c, direction, 2)

    pl.semaphore_wait(met.at[1], 2)
    greet(2)

    for copy in yx:
        copy.wait_recv()
    lin.wait_recv()
    total = lbuf[pl.ds(mine, half), :] + la[...]
    for part in split3(ybuf[...] + yin[...]):
        total = total + dot(xbuf[pl.ds(mine, half), :], part)
    lc[...] = total
    q = half // (N * N)

    def part_of(o):
        return pl.ds(pl.multiple_of((wrap(px + o[0]) * N + wrap(py + o[1])) * q, q), q)

    bins = [send(lc.at[part_of(o)], lx.at[i], c2s.at[2 + i], c2r.at[2 + i], away(o)) for i, o in enumerate(same)]
    stage2(0, 0)
    stage2(1, 0)
    stage2(0, 1)
    stage2(1, 1)
    stage3(0, 0)
    stage3(1, 0)
    total = lc[part_of((0, 0)), :]
    for i, copy in enumerate(bins):
        copy.wait_recv()
        total = total + lx[i]
    lfull[core, px, py] = total
    own = lfull.at[core, px, py]
    dins = [send(own, own, c2s.at[17 + i], c2r.at[17 + i], away(o)) for i, o in enumerate(same)]
    stage2(0, 2)
    stage2(1, 2)
    stage3(0, 1)
    stage3(1, 1)
    for copy in dins:
        copy.wait_recv()
    own = lfull.at[core]
    fin = send(own, own, c2s.at[32], c2r.at[32], sibling)
    for f in range(2):
        stage3(f, 2)
    pl.semaphore_wait(met.at[2], 2)
    fin.wait_recv()
    gin.wait_recv()

    low = lfull[...].reshape(rows, lanes)
    lt = low.T
    gm = (gram[0] + gram[1])[:, 0:64]
    xa = lt[64:64 + rank]
    xv = [lt[64 + rank * (i + 1):64 + rank * (i + 2)] for i in range(2)]
    zero16 = jnp.zeros((rank, rows), F32)
    hp = lt[0:64] + SCALE * dot(gm, jnp.concatenate([xa, zero16, zero16, zero16], 0), precision=HI)
    hb = hp[0:rank]
    hg = hp[48:56] + hp[56:64]
    gm8 = gm[48:56] + gm[56:64]
    stacks = [
        jnp.concatenate([xv[0], xa, zero16, zero16], 0),
        jnp.concatenate([xv[1], zero16, xa, zero16], 0),
    ]
    dhg = [SCALE * dot(gm8, st, precision=HI) for st in stacks]
    mk = [
        SCALE / model * jnp.sum(xv[i] * hb + xa * hp[rank * (i + 1):rank * (i + 2)], 0, keepdims=True)
        for i in range(2)
    ]
    prior = jnp.concatenate([prior_ref[...], jnp.zeros((4, rows), F32)], 0)

    xa_cols = [part for part in split3(low)]
    shift = (
        lax.broadcasted_iota(jnp.int32, (lanes, rank), 0) == lax.broadcasted_iota(jnp.int32, (lanes, rank), 1) + 64
    ).astype(F32).astype(BF16)
    spread = dot(shift, b_ref[...]).astype(BF16)
    ssend[...] = jnp.zeros_like(ssend)
    for c in range(chunks):
        for f in range(2):
            for direction in range(2):
                wait_n(f, c, direction, 1)
                wait_n(f, c, direction, 2)
            at = slice(f * half + c * tc, f * half + (c + 1) * tc)
            ad = dot(xa_cols[0][at], spread) + dot(xa_cols[1][at], spread) + dot(xa_cols[2][at], spread)
            parts = []
            for part in range(2):
                parts.append(
                    tb[f, pos[f][0] * N + pos[f][1], part, c * tc:(c + 1) * tc, :].astype(F32)
                    + r2[f, c, part, 2].astype(F32)
                    + r2[f, c, 1 - part, 1].astype(F32)
                )
            h = jnp.concatenate(parts, 1) + rbuf[at, :].astype(F32) + SCALE * ad
            hi = h.astype(BF16)
            hhi[at, :] = hi
            hlo[at, :] = (h - hi.astype(F32)).astype(BF16)
            sq = h * h
            sq = sq[:, :lanes] + sq[:, lanes:]
            n = f * chunks + c
            ssend[n:n + 1, :] = jnp.sum(sq.T, 0, keepdims=True)

    ins = [send(ssend, sx.at[i], c3s.at[i], c3r.at[i], away(o)) for i, o in enumerate(plane)]
    for copy in sends[:-len(ins)]:
        copy.wait_send()
    late = len(sends) - len(ins)
    stot = ssend[...]
    for i, copy in enumerate(ins):
        copy.wait_recv()
        stot = stot + sx[i]
    square = jnp.concatenate([stot[i:i + 1, :] for i in range(2 * chunks)], 1)

    r = lax.rsqrt(square / model + EPS)
    r3 = r * r * r
    live = lax.broadcasted_iota(jnp.int32, (8, rows), 0) < 4
    logits = jnp.where(live, r * hg + prior, -1e30)
    ex = jnp.where(live, jnp.exp(logits - jnp.max(logits, 0, keepdims=True)), 0.0)
    p = ex / jnp.sum(ex, 0, keepdims=True)
    us, cs, t1 = [], [], []
    gcol = gm[0:rank]
    for i in range(2):
        dl = r * dhg[i] - r3 * mk[i] * hg
        q = p * (dl - jnp.sum(p * dl, 0, keepdims=True)) / total_tokens
        s = jnp.sum(q * hg, 0, keepdims=True) / model
        back = dot(gcol, jnp.concatenate([zero16, zero16, zero16, q, q], 0), precision=HI)
        us.append(SCALE * (r * back - r3 * s * hb))
        cs.append(r3 * s * xa)
        t1.append(dot(xa, r * q, NT, precision=HI))
    uu = jnp.concatenate(split3(jnp.concatenate(us, 0)), 0)
    cc = jnp.concatenate(split3(jnp.concatenate(cs, 0)), 0)
    n32 = 2 * rank

    def fold(m):
        return m[0:n32] + m[n32:2 * n32] + m[2 * n32:3 * n32]

    ggn = fold(dot(uu, xbuf[:, 0:piece]))
    ch = fold(dot(cc, hhi[...]) + dot(cc, hlo[...]))
    curv = SCALE * (dot(jnp.concatenate(t1, 0), g8[...], precision=HI) - ch)

    zw = 3 * lanes
    for i in range(4):
        at = slice(8 * i, 8 * i + 8)
        zpart[2 * i] = ggn[at, 0:zw]
        zpart[2 * i + 1, :, 0:piece - zw] = ggn[at, zw:piece]
        zpart[2 * i + 1, :, lanes:zw] = curv[at, :]
    ins = []
    for o in zorder:
        ins.append(send(zpart.at[lax.rem(zi + o, zs)], zrecv.at[o - 1], zss.at[0, o - 1], zsr.at[0, o - 1], zpeer[o]))
    for copy in ins:
        copy.wait_recv()
    total = zpart[zi]
    for o in range(1, zs):
        total = total + zrecv[o - 1]
    zfull[zi] = total
    ins = [
        send(zfull.at[zi], zfull.at[zi], zss.at[1, o - 1], zsr.at[1, o - 1], zpeer[o]) for o in zorder
    ]
    for copy in ins:
        copy.wait_recv()
    out_ref[...] = zfull[...]
    for copy in sends[late:]:
        copy.wait_send()


def unpack(in_ref, ggn_ref, curv_ref):
    zw = in_ref.shape[2]
    piece = ggn_ref.shape[1]
    for i in range(4):
        at = slice(8 * i, 8 * i + 8)
        ggn_ref[at, 0:zw] = in_ref[2 * i]
        ggn_ref[at, zw:piece] = in_ref[2 * i + 1, :, 0:piece - zw]
        curv_ref[at, :] = in_ref[2 * i + 1, :, 128:zw]


def shards(zs, x, res, w, a_in, b_out, gain, head, prior, v_in, d_out):
    rows, piece = x.shape
    fb = res.shape[1]
    rank = a_in.shape[0]
    k = v_in.shape[0]
    chunks = 3
    half = rows // 2
    tc = half // chunks
    q = half // N // N
    vmem = pl.BlockSpec(memory_space=pltpu.VMEM)
    hbm = pl.BlockSpec(memory_space=pl.ANY)
    dma = pltpu.SemaphoreType.DMA
    packed = pl.pallas_call(
        functools.partial(kernel, chunks, zs, rows * zs),
        out_shape=jax.ShapeDtypeStruct((8, 8, 384), F32),
        in_specs=[hbm] * 10,
        out_specs=vmem,
        scratch_shapes=[
            pltpu.VMEM(a_in.shape, BF16),
            pltpu.VMEM(b_out.shape, BF16),
            pltpu.VMEM(gain.shape, BF16),
            pltpu.VMEM(head.shape, BF16),
            pltpu.VMEM((prior.shape[1], rows), F32),
            pltpu.VMEM((k * rank, piece), BF16),
            pltpu.VMEM((k * rank, fb), BF16),
            dma((7,)),
            pltpu.VMEM((2 * piece, rows), BF16),
            pltpu.VMEM((rows, 2 * piece), BF16),
            pltpu.VMEM((rows, fb), BF16),
            pltpu.VMEM((N * N, 2 * piece, fb), BF16),
            pltpu.VMEM((2, N * N, 2, half, 128), BF16),
            pltpu.VMEM((2, chunks, 2, 3, 2, 2, tc, 128), BF16),
            pltpu.VMEM((2, chunks, 2, 3, tc, 128), BF16),
            pltpu.VMEM((N, N, 128, fb), BF16),
            pltpu.VMEM((128, fb), BF16),
            pltpu.VMEM((8, fb), F32),
            pltpu.VMEM((128, piece), BF16),
            pltpu.VMEM((2 * piece, 128), F32),
            pltpu.VMEM((2 * piece, 128), F32),
            pltpu.VMEM((2, 64, 128), F32),
            pltpu.VMEM((rows, 128), F32),
            pltpu.VMEM((half, 128), F32),
            pltpu.VMEM((half, 128), F32),
            pltpu.VMEM((N * N - 1, q, 128), F32),
            pltpu.VMEM((2, N, N, q, 128), F32),
            pltpu.VMEM((rows, fb), BF16),
            pltpu.VMEM((rows, fb), BF16),
            pltpu.VMEM((8, 128), F32),
            pltpu.VMEM((2 * N * N - 1, 8, 128), F32),
            pltpu.VMEM((8, 8, 384), F32),
            pltpu.VMEM((zs - 1, 8, 384), F32),
            pltpu.VMEM((8, 8, 384), F32),
            dma((N * N,)), dma((2,)), dma((1,)),
            dma((N * N,)), dma((N * N,)), dma((2,)), dma((2,)),
            dma((2, chunks, 2, 3)), dma((2, chunks, 2, 3)),
            dma((2, chunks, 2, 3)), dma((2, chunks, 2, 3)),
            dma((7,)), dma((7,)),
            dma((35,)), dma((35,)), dma((2 * N * N - 1,)), dma((2 * N * N - 1,)),
            dma((2, zs - 1)), dma((2, zs - 1)),
            pltpu.SemaphoreType.REGULAR((3,)),
        ],
        compiler_params=pltpu.CompilerParams(
            collective_id=0, has_side_effects=True, vmem_limit_bytes=56 * 1024 * 1024
        ),
    )(
        x.T, res, w, a_in, b_out, gain, head, prior.T,
        v_in.reshape(k * rank, piece), d_out.reshape(k * rank, fb),
    )
    ggn, curv = pl.pallas_call(
        unpack,
        out_shape=(
            jax.ShapeDtypeStruct((k * rank, piece), F32),
            jax.ShapeDtypeStruct((k * rank, fb), F32),
        ),
    )(packed)
    return ggn.reshape(k, rank, piece), curv.reshape(k, rank, fb)


def solution(mesh):
    placed = (
        P("item", "tensor"),
        P("item", "tensor"),
        P("tensor", None),
        P(None, "tensor"),
        P(None, "tensor"),
        P("tensor"),
        P(None, "tensor"),
        P("item", None),
        P(None, None, "tensor"),
        P(None, None, "tensor"),
    )
    return jax.shard_map(
        functools.partial(shards, mesh.shape["item"]),
        mesh=mesh,
        in_specs=placed,
        out_specs=(P(None, None, "tensor"), P(None, None, "tensor")),
        check_vma=False,
    )
```

```python
import functools

import jax
import jax.numpy as jnp
from jax import lax
from jax.experimental import pallas as pl
from jax.experimental.pallas import tpu as pltpu
from jax.sharding import PartitionSpec as P

SCALE = 2.0
EPS = 1e-05
HI = lax.Precision.HIGHEST
F32 = jnp.float32
BF16 = jnp.bfloat16
N = 4
NT = (((1,), (1,)), ((), ()))
NN = (((1,), (0,)), ((), ()))


def dot(a, b, dims=NN, precision=None):
    return lax.dot_general(a, b, dims, preferred_element_type=F32, precision=precision)


def split3(v):
    a = v.astype(BF16)
    rest = v - a.astype(F32)
    b = rest.astype(BF16)
    c = (rest - b.astype(F32)).astype(BF16)
    return a, b, c


def wrap(v):
    return lax.rem(v, N)


def kernel(
    chunks, zs, total_tokens,
    x_hbm, r_hbm, w_hbm, a_hbm, b_hbm, g_hbm, head_hbm, prior_hbm, v_hbm, d_hbm,
    out_ref,
    a_ref, b_ref, g_ref, head_ref, prior_ref, v_ref, d_ref, sl,
    xt, xbuf, rbuf, wbuf, tb, r1, r2, pf, pown, g8, avp, ybuf, yin, gram, lbuf, la, lc, lx, lfull,
    hhi, hlo, ssend, sx, zpart, zrecv, zfull,
    wl, xl, rl, ws, wr, xs, xr, ms, mr, ns, nr, c1s, c1r, c2s, c2r, c3s, c3r, zss, zsr, met,
):
    piece, rows = x_hbm.shape
    half = rows // 2
    tc = half // chunks
    fb = r_hbm.shape[1]
    lanes = 128
    model = w_hbm.shape[1]
    rank = a_hbm.shape[0]
    zi = lax.axis_index("item")
    me = lax.axis_index("tensor")
    core = lax.rem(me, 2)
    chip = lax.div(me, 2)
    px = lax.div(chip, N)
    py = lax.rem(chip, N)

    def device(x, y, c):
        return {"tensor": (x * N + y) * 2 + c}

    sibling = device(px, py, 1 - core)
    xpeer = [None] + [device(wrap(px + o), py, core) for o in range(1, N)]
    ypeer = [None] + [device(px, wrap(py + o), core) for o in range(1, N)]
    zpeer = [None] + [{"item": lax.rem(zi + o, zs)} for o in range(1, zs)]

    def far(i, j, c=0):
        return min(i, N - i) + min(j, N - j) + 0.1 * c

    plane = [(i, j, c) for i in range(N) for j in range(N) for c in range(2)][1:]
    plane.sort(key=lambda o: -far(*o))
    same = [o for o in plane if o[2] == 0]
    zorder = sorted(range(1, zs), key=lambda o: -min(o, zs - o))

    def away(o):
        return device(wrap(px + o[0]), wrap(py + o[1]), lax.rem(core + o[2], 2))

    pa, pb = px + core * (py - px), py + core * (px - py)
    apeer = [None] + [device(wrap(px + o * (1 - core)), wrap(py + o * core), core) for o in range(1, N)]
    bpeer = [None] + [device(wrap(px + o * core), wrap(py + o * (1 - core)), core) for o in range(1, N)]

    def index(i, j, c):
        return i * (N - (N - 1) * c) + j * (1 + (N - 1) * c)

    sends = []

    def send(src, dst, ssem, rsem, to):
        copy = pltpu.make_async_remote_copy(
            src_ref=src, dst_ref=dst, send_sem=ssem, recv_sem=rsem,
            device_id=to, device_id_type=pl.DeviceIdType.MESH,
        )
        copy.start()
        sends.append(copy)
        return copy

    barrier = pltpu.get_barrier_semaphore()
    peers = [sibling] + xpeer[1:] + ypeer[1:] + [zpeer[1], zpeer[zs - 1]]
    for to in peers:
        pl.semaphore_signal(barrier, inc=1, device_id=to, device_id_type=pl.DeviceIdType.MESH)

    order = [(2, o) for o in range(N)] + [(o, 2) for o in (0, 1, 3)]
    order += [(i, j) for i in (1, 3, 0) for j in (3, 0, 1)]

    def block(n):
        if n < N:
            return index(wrap(pa + 2), n, core)
        return index(wrap(pa + order[n][0]), wrap(pb + order[n][1]), core)

    def other_block(n):
        if n < N:
            return index(wrap(pb + 2), n, 1 - core)
        return index(wrap(pb + order[n][0]), wrap(pa + order[n][1]), 1 - core)

    def columns(b, c):
        return pl.ds(pl.multiple_of((b * 2 + c) * fb, fb), fb)

    xloads = [
        pltpu.make_async_copy(x_hbm.at[:, pl.ds(f * half, half)], xt.at[pl.ds(0, piece), pl.ds(f * half, half)], xl.at[f])
        for f in range(2)
    ]
    wloads = [
        pltpu.make_async_copy(w_hbm.at[:, columns(block(n), core)], wbuf.at[block(n), pl.ds(0, piece)], wl.at[n])
        for n in range(N * N)
    ]
    small = [
        pltpu.make_async_copy(src, dst, sl.at[i])
        for i, (src, dst) in enumerate([
            (b_hbm, b_ref), (d_hbm, d_ref), (g_hbm, g_ref), (head_hbm, head_ref), (a_hbm, a_ref), (v_hbm, v_ref),
            (prior_hbm, prior_ref),
        ])
    ]
    rload = pltpu.make_async_copy(r_hbm, rbuf, rl.at[0])
    for copy in small:
        copy.start()
    xloads[0].start()
    for n in range(N):
        wloads[n].start()
    xloads[1].start()
    for n in range(N, N * N):
        wloads[n].start()
    rload.start()
    for copy in small:
        copy.wait()

    g8[...] = jnp.zeros_like(g8)
    g8[0:4, :] = head_ref[...].astype(F32) * g_ref[...].astype(F32).reshape(1, fb)
    ghi = g8[...].astype(BF16).astype(F32)
    pf[:, :, 64:128, :] = jnp.zeros((N, N, 64, fb), BF16)
    pown[64:128, :] = jnp.zeros((64, fb), BF16)
    pown[0:rank, :] = b_ref[...]
    pown[rank:3 * rank, :] = d_ref[...]
    pown[3 * rank:64, :] = jnp.concatenate([ghi, g8[...] - ghi], 0).astype(BF16)
    avp[...] = jnp.zeros_like(avp)
    avp[64:64 + rank, :] = a_ref[...]
    avp[64 + rank:64 + 3 * rank, :] = v_ref[...]

    share = pl.ds(pl.multiple_of(lax.rem(zi, 2) * 32, 32), 32)
    pf[pb, pa, share, :] = pown[share, :]
    pl.semaphore_wait(barrier, len(peers))

    def send_x(f):
        return send(x_hbm.at[:, pl.ds(f * half, half)], xt.at[pl.ds(piece, piece), pl.ds(f * half, half)], xs.at[f], xr.at[f], sibling)

    def send_w(n):
        return send(w_hbm.at[:, columns(other_block(n), 1 - core)], wbuf.at[other_block(n), pl.ds(piece, piece)], ws.at[n], wr.at[n], sibling)

    xin = [send_x(0)]
    win = [send_w(n) for n in range(N)]
    pin = [
        send(pown.at[share], pf.at[pb, pa, share], c1s.at[o - 1], c1r.at[o - 1], apeer[o]) for o in (2, 1, 3)
    ]
    xin.append(send_x(1))
    win += [send_w(n) for n in range(N, N * N)]

    def recv_slot(src_shape_ref, sem):
        return pltpu.make_async_copy(src_shape_ref, src_shape_ref, sem)

    pos = [(pa, pb), (pb, pa)]

    eye = (
        lax.broadcasted_iota(jnp.int32, (lanes, lanes), 0) == lax.broadcasted_iota(jnp.int32, (lanes, lanes), 1)
    ).astype(F32).astype(BF16)

    def turn(f):
        for i in range(half // lanes):
            at = slice(f * half + i * lanes, f * half + (i + 1) * lanes)
            xbuf[at, :] = dot(eye, xt[:, at], NT).astype(BF16)

    def put(f, i1, i2, out):
        tb[f, i1 * N + i2, 0] = out[:, :lanes]
        tb[f, i1 * N + i2, 1] = out[:, lanes:]

    def group(f, i1, lo=0, hi=N):
        def body(i2, carry):
            b = index(i1, i2, core) if f == 0 else index(i2, i1, core)
            put(f, i1, i2, dot(xbuf[f * half:(f + 1) * half, :], wbuf[b]).astype(BF16))
            return carry

        lax.fori_loop(lo, hi, body, 0)

    def both(count, ox, oy):
        def body(n, carry):
            x, y = wrap(pa + ox(n)), wrap(pb + oy(n))
            out = dot(xbuf[...], wbuf[index(x, y, core)]).astype(BF16)
            put(0, x, y, out[:half])
            put(1, y, x, out[half:])
            return carry

        lax.fori_loop(0, count, body, 0)

    def single(f, offsets):
        def body(n, carry):
            i1, i2 = wrap(pos[f][0] + offsets(n)), wrap(pos[f][1] + 2)
            b = index(i1, i2, core) if f == 0 else index(i2, i1, core)
            put(f, i1, i2, dot(xbuf[f * half:(f + 1) * half, :], wbuf[b]).astype(BF16))
            return carry

        return body

    def send_m(f, c, direction, msg):
        peer = apeer if f == 0 else bpeer
        to = peer[1] if direction == 0 else peer[N - 1]
        offset = 2 if msg == 0 else (1 if direction == 0 else N - 1)
        i1 = wrap(pos[f][0] + offset)
        part = 1 - direction if msg == 1 else direction
        send(
            tb.at[f, pl.ds(i1 * N + 2 * part, 2), :, pl.ds(c * tc, tc), :],
            r1.at[f, c, direction, msg],
            ms.at[f, c, direction, msg], mr.at[f, c, direction, msg], to,
        )

    def wait_m(f, c, direction, msg):
        recv_slot(r1.at[f, c, direction, msg], mr.at[f, c, direction, msg]).wait()

    def send_n(f, c, direction, msg):
        peer = bpeer if f == 0 else apeer
        to = peer[1] if direction == 0 else peer[N - 1]
        offset = 2 if msg == 0 else (1 if direction == 0 else N - 1)
        i2 = wrap(pos[f][1] + offset)
        part = 1 - direction if msg == 1 else direction
        send(
            tb.at[f, pos[f][0] * N + i2, part, pl.ds(c * tc, tc), :],
            r2.at[f, c, direction, msg],
            ns.at[f, c, direction, msg], nr.at[f, c, direction, msg], to,
        )

    def wait_n(f, c, direction, msg):
        recv_slot(r2.at[f, c, direction, msg], nr.at[f, c, direction, msg]).wait()

    def wait_w(n):
        wloads[n].wait()
        recv_slot(wbuf.at[block(n), pl.ds(piece, piece)], wr.at[n]).wait()

    def first(f):
        xloads[f].wait()
        xin[f].wait_recv()
        turn(f)

    def start(f):
        for direction in range(2):
            if f == 0:
                wait_w(2 * direction)
                wait_w(2 * direction + 1)
            group(f, wrap(pos[f][0] + 2), 2 * direction, 2 * direction + 2)
            for c in range(chunks):
                send_m(f, c, direction, 0)

    first(0)
    start(0)
    for copy in pin:
        copy.wait_recv()
    pin = [
        send(pf.at[pb, :, share], pf.at[pb, :, share], c1s.at[2 + o], c1r.at[2 + o], bpeer[o]) for o in (2, 1, 3)
    ]
    first(1)
    for n in range(N, 2 * N - 1):
        wait_w(n)
    start(1)

    def greet(n):
        for to in (zpeer[1], zpeer[zs - 1]):
            pl.semaphore_signal(met.at[n], inc=1, device_id=to, device_id_type=pl.DeviceIdType.MESH)

    greet(0)
    def send_m2(f, c):
        for direction in range(2):
            send_m(f, c, direction, 1)

    for i, o in enumerate((1, 3)):
        for n in range(2 * N - 1 + 3 * i, 2 * N + 2 + 3 * i):
            wait_w(n)
        both(3, lambda n: o, lambda n: N - 1 + n)
        lax.fori_loop(0, 1, single(0, lambda n: o + n), 0)
        send_m(0, 0, i, 1)
    for copy in pin:
        copy.wait_recv()
    pair = {"item": zi + 1 - 2 * lax.rem(zi, 2)}
    pin = [send(pf.at[:, :, share], pf.at[:, :, share], c1s.at[6], c1r.at[6], pair)]
    for n in range(N * N - 3, N * N):
        wait_w(n)
    for i, o in enumerate((1, 3)):
        both(1, lambda n: n, lambda n: o + n)
        lax.fori_loop(0, 1, single(1, lambda n: o + n), 0)
        send_m(1, 0, i, 1)

    def middle(f, c):
        for direction in range(2):
            wait_m(f, c, direction, 0)
            i1 = wrap(pos[f][0] + (1 if direction == 0 else N - 1))
            at = (f, pl.ds(i1 * N + 2 * direction, 2), slice(None), pl.ds(c * tc, tc), slice(None))
            tb[at] = (tb[at].astype(F32) + r1[f, c, direction, 0].astype(F32)).astype(BF16)
            send_m(f, c, direction, 2)

    for f in range(2):
        middle(f, 0)
        send_m2(f, 1)
    both(1, lambda n: n, lambda n: n)
    for f in range(2):
        lax.fori_loop(0, 1, single(f, lambda n: n), 0)
    for f in range(2):
        middle(f, 1)
        send_m2(f, 2)
    for f in range(2):
        middle(f, 2)

    pl.semaphore_wait(met.at[0], 2)
    greet(1)

    for copy in pin:
        copy.wait_recv()
    for i in range(piece // 64):
        at = slice(i * 64, (i + 1) * 64)
        ybuf[at, :] = dot(eye[0:64, 0:64], avp[:, at], NT)
    ybuf[piece:, :] = jnp.zeros((piece, lanes), F32)
    gram[0] = jnp.zeros((64, lanes), F32)

    def project(j, carry):
        acc, g = 0.0, 0.0
        for i in range(N):
            p = pf[j, i]
            acc = acc + dot(wbuf[index(i, j, core)], p, NT)
            g = g + dot(p[0:64], p, NT)
        ybuf[...] = ybuf[...] + acc
        gram[0] = gram[0] + g
        return carry

    lax.fori_loop(0, N, project, 0)
    yx = [
        send(ybuf.at[pl.ds(s * piece, piece)], yin.at[pl.ds((1 - s) * piece, piece)], c2s.at[33 + s], c2r.at[33 + s], sibling)
        for s in range(2)
    ]
    gin = send(gram.at[0], gram.at[1], c2s.at[1], c2r.at[1], sibling)
    other = pl.multiple_of((1 - core) * half, half)
    mine = pl.multiple_of(core * half, half)
    rload.wait()
    lbuf[...] = dot(rbuf[...], pown[...], NT)
    lin = send(lbuf.at[pl.ds(other, half)], la, c2s.at[0], c2r.at[0], sibling)

    def stage2(f, c):
        wait_m(f, c, 0, 1)
        wait_m(f, c, 1, 1)
        wait_m(f, c, 0, 2)
        wait_m(f, c, 1, 2)
        for part in range(2):
            at = (f, pl.ds(pos[f][0] * N + 2 * part, 2), slice(None), pl.ds(c * tc, tc), slice(None))
            tb[at] = (
                tb[at].astype(F32)
                + r1[f, c, part, 2].astype(F32)
                + r1[f, c, 1 - part, 1].astype(F32)
            ).astype(BF16)
        for msg in range(2):
            for direction in range(2):
                send_n(f, c, direction, msg)

    def stage3(f, c):
        for direction in range(2):
            wait_n(f, c, direction, 0)
            i2 = wrap(pos[f][1] + (1 if direction == 0 else N - 1))
            at = (f, pos[f][0] * N + i2, direction, pl.ds(c * tc, tc), slice(None))
            tb[at] = (tb[at].astype(F32) + r2[f, c, direction, 0].astype(F32)).astype(BF16)
            send_n(f, c, direction, 2)

    pl.semaphore_wait(met.at[1], 2)
    greet(2)

    for copy in yx:
        copy.wait_recv()
    lin.wait_recv()
    total = lbuf[pl.ds(mine, half), :] + la[...]
    for part in split3(ybuf[...] + yin[...]):
        total = total + dot(xbuf[pl.ds(mine, half), :], part)
    lc[...] = total
    q = half // (N * N)

    def part_of(o):
        return pl.ds(pl.multiple_of((wrap(px + o[0]) * N + wrap(py + o[1])) * q, q), q)

    bins = [send(lc.at[part_of(o)], lx.at[i], c2s.at[2 + i], c2r.at[2 + i], away(o)) for i, o in enumerate(same)]
    stage2(0, 0)
    stage2(1, 0)
    stage2(0, 1)
    stage2(1, 1)
    total = lc[part_of((0, 0)), :]
    for i, copy in enumerate(bins):
        copy.wait_recv()
        total = total + lx[i]
    lfull[core, px, py] = total
    own = lfull.at[core, px, py]
    dins = [send(own, own, c2s.at[17 + i], c2r.at[17 + i], away(o)) for i, o in enumerate(same)]
    stage3(0, 0)
    stage3(1, 0)
    stage2(0, 2)
    stage2(1, 2)
    stage3(0, 1)
    stage3(1, 1)
    for copy in dins:
        copy.wait_recv()
    own = lfull.at[core]
    fin = send(own, own, c2s.at[32], c2r.at[32], sibling)
    for f in range(2):
        stage3(f, 2)
    pl.semaphore_wait(met.at[2], 2)
    fin.wait_recv()
    gin.wait_recv()

    low = lfull[...].reshape(rows, lanes)
    lt = low.T
    gm = (gram[0] + gram[1])[:, 0:64]
    xa = lt[64:64 + rank]
    xv = [lt[64 + rank * (i + 1):64 + rank * (i + 2)] for i in range(2)]
    zero16 = jnp.zeros((rank, rows), F32)
    hp = lt[0:64] + SCALE * dot(gm, jnp.concatenate([xa, zero16, zero16, zero16], 0), precision=HI)
    hb = hp[0:rank]
    hg = hp[48:56] + hp[56:64]
    gm8 = gm[48:56] + gm[56:64]
    stacks = [
        jnp.concatenate([xv[0], xa, zero16, zero16], 0),
        jnp.concatenate([xv[1], zero16, xa, zero16], 0),
    ]
    dhg = [SCALE * dot(gm8, st, precision=HI) for st in stacks]
    mk = [
        SCALE / model * jnp.sum(xv[i] * hb + xa * hp[rank * (i + 1):rank * (i + 2)], 0, keepdims=True)
        for i in range(2)
    ]
    prior = jnp.concatenate([prior_ref[...], jnp.zeros((4, rows), F32)], 0)

    xa_cols = [part for part in split3(low)]
    shift = (
        lax.broadcasted_iota(jnp.int32, (lanes, rank), 0) == lax.broadcasted_iota(jnp.int32, (lanes, rank), 1) + 64
    ).astype(F32).astype(BF16)
    spread = dot(shift, b_ref[...]).astype(BF16)
    ssend[...] = jnp.zeros_like(ssend)
    for c in range(chunks):
        for f in range(2):
            for direction in range(2):
                wait_n(f, c, direction, 1)
                wait_n(f, c, direction, 2)
            at = slice(f * half + c * tc, f * half + (c + 1) * tc)
            ad = dot(xa_cols[0][at], spread) + dot(xa_cols[1][at], spread) + dot(xa_cols[2][at], spread)
            parts = []
            for part in range(2):
                parts.append(
                    tb[f, pos[f][0] * N + pos[f][1], part, c * tc:(c + 1) * tc, :].astype(F32)
                    + r2[f, c, part, 2].astype(F32)
                    + r2[f, c, 1 - part, 1].astype(F32)
                )
            h = jnp.concatenate(parts, 1) + rbuf[at, :].astype(F32) + SCALE * ad
            hi = h.astype(BF16)
            hhi[at, :] = hi
            hlo[at, :] = (h - hi.astype(F32)).astype(BF16)
            sq = h * h
            sq = sq[:, :lanes] + sq[:, lanes:]
            n = f * chunks + c
            ssend[n:n + 1, :] = jnp.sum(sq.T, 0, keepdims=True)

    ins = [send(ssend, sx.at[i], c3s.at[i], c3r.at[i], away(o)) for i, o in enumerate(plane)]
    for copy in sends[:-len(ins)]:
        copy.wait_send()
    late = len(sends) - len(ins)
    stot = ssend[...]
    for i, copy in enumerate(ins):
        copy.wait_recv()
        stot = stot + sx[i]
    square = jnp.concatenate([stot[i:i + 1, :] for i in range(2 * chunks)], 1)

    r = lax.rsqrt(square / model + EPS)
    r3 = r * r * r
    live = lax.broadcasted_iota(jnp.int32, (8, rows), 0) < 4
    logits = jnp.where(live, r * hg + prior, -1e30)
    ex = jnp.where(live, jnp.exp(logits - jnp.max(logits, 0, keepdims=True)), 0.0)
    p = ex / jnp.sum(ex, 0, keepdims=True)
    us, cs, t1 = [], [], []
    gcol = gm[0:rank]
    for i in range(2):
        dl = r * dhg[i] - r3 * mk[i] * hg
        q = p * (dl - jnp.sum(p * dl, 0, keepdims=True)) / total_tokens
        s = jnp.sum(q * hg, 0, keepdims=True) / model
        back = dot(gcol, jnp.concatenate([zero16, zero16, zero16, q, q], 0), precision=HI)
        us.append(SCALE * (r * back - r3 * s * hb))
        cs.append(r3 * s * xa)
        t1.append(dot(xa, r * q, NT, precision=HI))
    uu = jnp.concatenate(split3(jnp.concatenate(us, 0)), 0)
    cc = jnp.concatenate(split3(jnp.concatenate(cs, 0)), 0)
    n32 = 2 * rank

    def fold(m):
        return m[0:n32] + m[n32:2 * n32] + m[2 * n32:3 * n32]

    ggn = fold(dot(uu, xbuf[:, 0:piece]))
    ch = fold(dot(cc, hhi[...]) + dot(cc, hlo[...]))
    curv = SCALE * (dot(jnp.concatenate(t1, 0), g8[...], precision=HI) - ch)

    zw = 3 * lanes
    for i in range(4):
        at = slice(8 * i, 8 * i + 8)
        zpart[2 * i] = ggn[at, 0:zw]
        zpart[2 * i + 1, :, 0:piece - zw] = ggn[at, zw:piece]
        zpart[2 * i + 1, :, lanes:zw] = curv[at, :]
    ins = []
    for o in zorder:
        ins.append(send(zpart.at[lax.rem(zi + o, zs)], zrecv.at[o - 1], zss.at[0, o - 1], zsr.at[0, o - 1], zpeer[o]))
    for copy in ins:
        copy.wait_recv()
    total = zpart[zi]
    for o in range(1, zs):
        total = total + zrecv[o - 1]
    zfull[zi] = total
    ins = [
        send(zfull.at[zi], zfull.at[zi], zss.at[1, o - 1], zsr.at[1, o - 1], zpeer[o]) for o in zorder
    ]
    for copy in ins:
        copy.wait_recv()
    out_ref[...] = zfull[...]
    for copy in sends[late:]:
        copy.wait_send()


def unpack(in_ref, ggn_ref, curv_ref):
    zw = in_ref.shape[2]
    piece = ggn_ref.shape[1]
    for i in range(4):
        at = slice(8 * i, 8 * i + 8)
        ggn_ref[at, 0:zw] = in_ref[2 * i]
        ggn_ref[at, zw:piece] = in_ref[2 * i + 1, :, 0:piece - zw]
        curv_ref[at, :] = in_ref[2 * i + 1, :, 128:zw]


def shards(zs, x, res, w, a_in, b_out, gain, head, prior, v_in, d_out):
    rows, piece = x.shape
    fb = res.shape[1]
    rank = a_in.shape[0]
    k = v_in.shape[0]
    chunks = 3
    half = rows // 2
    tc = half // chunks
    q = half // N // N
    vmem = pl.BlockSpec(memory_space=pltpu.VMEM)
    hbm = pl.BlockSpec(memory_space=pl.ANY)
    dma = pltpu.SemaphoreType.DMA
    packed = pl.pallas_call(
        functools.partial(kernel, chunks, zs, rows * zs),
        out_shape=jax.ShapeDtypeStruct((8, 8, 384), F32),
        in_specs=[hbm] * 10,
        out_specs=vmem,
        scratch_shapes=[
            pltpu.VMEM(a_in.shape, BF16),
            pltpu.VMEM(b_out.shape, BF16),
            pltpu.VMEM(gain.shape, BF16),
            pltpu.VMEM(head.shape, BF16),
            pltpu.VMEM((prior.shape[1], rows), F32),
            pltpu.VMEM((k * rank, piece), BF16),
            pltpu.VMEM((k * rank, fb), BF16),
            dma((7,)),
            pltpu.VMEM((2 * piece, rows), BF16),
            pltpu.VMEM((rows, 2 * piece), BF16),
            pltpu.VMEM((rows, fb), BF16),
            pltpu.VMEM((N * N, 2 * piece, fb), BF16),
            pltpu.VMEM((2, N * N, 2, half, 128), BF16),
            pltpu.VMEM((2, chunks, 2, 3, 2, 2, tc, 128), BF16),
            pltpu.VMEM((2, chunks, 2, 3, tc, 128), BF16),
            pltpu.VMEM((N, N, 128, fb), BF16),
            pltpu.VMEM((128, fb), BF16),
            pltpu.VMEM((8, fb), F32),
            pltpu.VMEM((128, piece), BF16),
            pltpu.VMEM((2 * piece, 128), F32),
            pltpu.VMEM((2 * piece, 128), F32),
            pltpu.VMEM((2, 64, 128), F32),
            pltpu.VMEM((rows, 128), F32),
            pltpu.VMEM((half, 128), F32),
            pltpu.VMEM((half, 128), F32),
            pltpu.VMEM((N * N - 1, q, 128), F32),
            pltpu.VMEM((2, N, N, q, 128), F32),
            pltpu.VMEM((rows, fb), BF16),
            pltpu.VMEM((rows, fb), BF16),
            pltpu.VMEM((8, 128), F32),
            pltpu.VMEM((2 * N * N - 1, 8, 128), F32),
            pltpu.VMEM((8, 8, 384), F32),
            pltpu.VMEM((zs - 1, 8, 384), F32),
            pltpu.VMEM((8, 8, 384), F32),
            dma((N * N,)), dma((2,)), dma((1,)),
            dma((N * N,)), dma((N * N,)), dma((2,)), dma((2,)),
            dma((2, chunks, 2, 3)), dma((2, chunks, 2, 3)),
            dma((2, chunks, 2, 3)), dma((2, chunks, 2, 3)),
            dma((7,)), dma((7,)),
            dma((35,)), dma((35,)), dma((2 * N * N - 1,)), dma((2 * N * N - 1,)),
            dma((2, zs - 1)), dma((2, zs - 1)),
            pltpu.SemaphoreType.REGULAR((3,)),
        ],
        compiler_params=pltpu.CompilerParams(
            collective_id=0, has_side_effects=True, vmem_limit_bytes=56 * 1024 * 1024
        ),
    )(
        x.T, res, w, a_in, b_out, gain, head, prior.T,
        v_in.reshape(k * rank, piece), d_out.reshape(k * rank, fb),
    )
    ggn, curv = pl.pallas_call(
        unpack,
        out_shape=(
            jax.ShapeDtypeStruct((k * rank, piece), F32),
            jax.ShapeDtypeStruct((k * rank, fb), F32),
        ),
    )(packed)
    return ggn.reshape(k, rank, piece), curv.reshape(k, rank, fb)


def solution(mesh):
    placed = (
        P("item", "tensor"),
        P("item", "tensor"),
        P("tensor", None),
        P(None, "tensor"),
        P(None, "tensor"),
        P("tensor"),
        P(None, "tensor"),
        P("item", None),
        P(None, None, "tensor"),
        P(None, None, "tensor"),
    )
    return jax.shard_map(
        functools.partial(shards, mesh.shape["item"]),
        mesh=mesh,
        in_specs=placed,
        out_specs=(P(None, None, "tensor"), P(None, None, "tensor")),
        check_vma=False,
    )
```

```python
import functools

import jax
import jax.numpy as jnp
from jax import lax
from jax.experimental import pallas as pl
from jax.experimental.pallas import tpu as pltpu
from jax.sharding import PartitionSpec as P

SCALE = 2.0
EPS = 1e-05
HI = lax.Precision.HIGHEST
F32 = jnp.float32
BF16 = jnp.bfloat16
N = 4
NT = (((1,), (1,)), ((), ()))
NN = (((1,), (0,)), ((), ()))


def dot(a, b, dims=NN, precision=None):
    return lax.dot_general(a, b, dims, preferred_element_type=F32, precision=precision)


def split3(v):
    a = v.astype(BF16)
    rest = v - a.astype(F32)
    b = rest.astype(BF16)
    c = (rest - b.astype(F32)).astype(BF16)
    return a, b, c


def wrap(v):
    return lax.rem(v, N)


def kernel(
    chunks, zs, total_tokens,
    x_hbm, r_hbm, w_hbm, a_hbm, b_hbm, g_hbm, head_hbm, prior_hbm, v_hbm, d_hbm,
    out_ref,
    a_ref, b_ref, g_ref, head_ref, prior_ref, v_ref, d_ref, sl,
    xt, xbuf, rbuf, wbuf, tb, r1, r2, pf, pown, g8, avp, ybuf, yin, gram, lbuf, la, lc, lx, lfull,
    hhi, hlo, ssend, sx, zpart, zrecv, zfull,
    wl, xl, rl, ws, wr, xs, xr, ms, mr, ns, nr, c1s, c1r, c2s, c2r, c3s, c3r, zss, zsr, met,
):
    piece, rows = x_hbm.shape
    half = rows // 2
    tc = half // chunks
    fb = r_hbm.shape[1]
    lanes = 128
    model = w_hbm.shape[1]
    rank = a_hbm.shape[0]
    zi = lax.axis_index("item")
    me = lax.axis_index("tensor")
    core = lax.rem(me, 2)
    chip = lax.div(me, 2)
    px = lax.div(chip, N)
    py = lax.rem(chip, N)

    def device(x, y, c):
        return {"tensor": (x * N + y) * 2 + c}

    sibling = device(px, py, 1 - core)
    xpeer = [None] + [device(wrap(px + o), py, core) for o in range(1, N)]
    ypeer = [None] + [device(px, wrap(py + o), core) for o in range(1, N)]
    zpeer = [None] + [{"item": lax.rem(zi + o, zs)} for o in range(1, zs)]

    def far(i, j, c=0):
        return min(i, N - i) + min(j, N - j) + 0.1 * c

    plane = [(i, j, c) for i in range(N) for j in range(N) for c in range(2)][1:]
    plane.sort(key=lambda o: -far(*o))
    same = [o for o in plane if o[2] == 0]
    zorder = sorted(range(1, zs), key=lambda o: -min(o, zs - o))

    def away(o):
        return device(wrap(px + o[0]), wrap(py + o[1]), lax.rem(core + o[2], 2))

    pa, pb = px + core * (py - px), py + core * (px - py)
    apeer = [None] + [device(wrap(px + o * (1 - core)), wrap(py + o * core), core) for o in range(1, N)]
    bpeer = [None] + [device(wrap(px + o * core), wrap(py + o * (1 - core)), core) for o in range(1, N)]

    def index(i, j, c):
        return i * (N - (N - 1) * c) + j * (1 + (N - 1) * c)

    sends = []

    def send(src, dst, ssem, rsem, to):
        copy = pltpu.make_async_remote_copy(
            src_ref=src, dst_ref=dst, send_sem=ssem, recv_sem=rsem,
            device_id=to, device_id_type=pl.DeviceIdType.MESH,
        )
        copy.start()
        sends.append(copy)
        return copy

    barrier = pltpu.get_barrier_semaphore()
    peers = [sibling] + xpeer[1:] + ypeer[1:] + [zpeer[1], zpeer[zs - 1]]
    for to in peers:
        pl.semaphore_signal(barrier, inc=1, device_id=to, device_id_type=pl.DeviceIdType.MESH)

    order = [(2, o) for o in range(N)] + [(o, 2) for o in (0, 1, 3)]
    order += [(i, j) for i in (1, 3, 0) for j in (3, 0, 1)]

    def block(n):
        if n < N:
            return index(wrap(pa + 2), n, core)
        return index(wrap(pa + order[n][0]), wrap(pb + order[n][1]), core)

    def other_block(n):
        if n < N:
            return index(wrap(pb + 2), n, 1 - core)
        return index(wrap(pb + order[n][0]), wrap(pa + order[n][1]), 1 - core)

    def columns(b, c):
        return pl.ds(pl.multiple_of((b * 2 + c) * fb, fb), fb)

    xloads = [
        pltpu.make_async_copy(x_hbm.at[:, pl.ds(f * half, half)], xt.at[pl.ds(0, piece), pl.ds(f * half, half)], xl.at[f])
        for f in range(2)
    ]
    wloads = [
        pltpu.make_async_copy(w_hbm.at[:, columns(block(n), core)], wbuf.at[block(n), pl.ds(0, piece)], wl.at[n])
        for n in range(N * N)
    ]
    small = [
        pltpu.make_async_copy(src, dst, sl.at[i])
        for i, (src, dst) in enumerate([
            (b_hbm, b_ref), (d_hbm, d_ref), (g_hbm, g_ref), (head_hbm, head_ref), (a_hbm, a_ref), (v_hbm, v_ref),
            (prior_hbm, prior_ref),
        ])
    ]
    rload = pltpu.make_async_copy(r_hbm, rbuf, rl.at[0])
    for copy in small:
        copy.start()
    xloads[0].start()
    for n in range(N):
        wloads[n].start()
    xloads[1].start()
    for n in range(N, N * N):
        wloads[n].start()
    rload.start()
    for copy in small:
        copy.wait()

    g8[...] = jnp.zeros_like(g8)
    g8[0:4, :] = head_ref[...].astype(F32) * g_ref[...].astype(F32).reshape(1, fb)
    ghi = g8[...].astype(BF16).astype(F32)
    pf[:, :, 64:128, :] = jnp.zeros((N, N, 64, fb), BF16)
    pown[64:128, :] = jnp.zeros((64, fb), BF16)
    pown[0:rank, :] = b_ref[...]
    pown[rank:3 * rank, :] = d_ref[...]
    pown[3 * rank:64, :] = jnp.concatenate([ghi, g8[...] - ghi], 0).astype(BF16)
    avp[...] = jnp.zeros_like(avp)
    avp[64:64 + rank, :] = a_ref[...]
    avp[64 + rank:64 + 3 * rank, :] = v_ref[...]

    share = pl.ds(pl.multiple_of(lax.rem(zi, 2) * 32, 32), 32)
    pf[pb, pa, share, :] = pown[share, :]
    pl.semaphore_wait(barrier, len(peers))

    def send_x(f):
        return send(x_hbm.at[:, pl.ds(f * half, half)], xt.at[pl.ds(piece, piece), pl.ds(f * half, half)], xs.at[f], xr.at[f], sibling)

    def send_w(n):
        return send(w_hbm.at[:, columns(other_block(n), 1 - core)], wbuf.at[other_block(n), pl.ds(piece, piece)], ws.at[n], wr.at[n], sibling)

    xin = [send_x(0)]
    win = [send_w(n) for n in range(N)]
    pin = [
        send(pown.at[share], pf.at[pb, pa, share], c1s.at[o - 1], c1r.at[o - 1], apeer[o]) for o in (2, 1, 3)
    ]
    xin.append(send_x(1))
    win += [send_w(n) for n in range(N, N * N)]

    def recv_slot(src_shape_ref, sem):
        return pltpu.make_async_copy(src_shape_ref, src_shape_ref, sem)

    pos = [(pa, pb), (pb, pa)]

    eye = (
        lax.broadcasted_iota(jnp.int32, (lanes, lanes), 0) == lax.broadcasted_iota(jnp.int32, (lanes, lanes), 1)
    ).astype(F32).astype(BF16)

    def turn(f):
        for i in range(half // lanes):
            at = slice(f * half + i * lanes, f * half + (i + 1) * lanes)
            xbuf[at, :] = dot(eye, xt[:, at], NT).astype(BF16)

    def put(f, i1, i2, out):
        tb[f, i1 * N + i2, 0] = out[:, :lanes]
        tb[f, i1 * N + i2, 1] = out[:, lanes:]

    def group(f, i1, lo=0, hi=N):
        def body(i2, carry):
            b = index(i1, i2, core) if f == 0 else index(i2, i1, core)
            put(f, i1, i2, dot(xbuf[f * half:(f + 1) * half, :], wbuf[b]).astype(BF16))
            return carry

        lax.fori_loop(lo, hi, body, 0)

    def both(count, ox, oy):
        def body(n, carry):
            x, y = wrap(pa + ox(n)), wrap(pb + oy(n))
            out = dot(xbuf[...], wbuf[index(x, y, core)]).astype(BF16)
            put(0, x, y, out[:half])
            put(1, y, x, out[half:])
            return carry

        lax.fori_loop(0, count, body, 0)

    def single(f, offsets):
        def body(n, carry):
            i1, i2 = wrap(pos[f][0] + offsets(n)), wrap(pos[f][1] + 2)
            b = index(i1, i2, core) if f == 0 else index(i2, i1, core)
            put(f, i1, i2, dot(xbuf[f * half:(f + 1) * half, :], wbuf[b]).astype(BF16))
            return carry

        return body

    def send_m(f, c, direction, msg):
        peer = apeer if f == 0 else bpeer
        to = peer[1] if direction == 0 else peer[N - 1]
        offset = 2 if msg == 0 else (1 if direction == 0 else N - 1)
        i1 = wrap(pos[f][0] + offset)
        part = 1 - direction if msg == 1 else direction
        send(
            tb.at[f, pl.ds(i1 * N + 2 * part, 2), :, pl.ds(c * tc, tc), :],
            r1.at[f, c, direction, msg],
            ms.at[f, c, direction, msg], mr.at[f, c, direction, msg], to,
        )

    def wait_m(f, c, direction, msg):
        recv_slot(r1.at[f, c, direction, msg], mr.at[f, c, direction, msg]).wait()

    def send_n(f, c, direction, msg):
        peer = bpeer if f == 0 else apeer
        to = peer[1] if direction == 0 else peer[N - 1]
        offset = 2 if msg == 0 else (1 if direction == 0 else N - 1)
        i2 = wrap(pos[f][1] + offset)
        part = 1 - direction if msg == 1 else direction
        send(
            tb.at[f, pos[f][0] * N + i2, part, pl.ds(c * tc, tc), :],
            r2.at[f, c, direction, msg],
            ns.at[f, c, direction, msg], nr.at[f, c, direction, msg], to,
        )

    def wait_n(f, c, direction, msg):
        recv_slot(r2.at[f, c, direction, msg], nr.at[f, c, direction, msg]).wait()

    def wait_w(n):
        wloads[n].wait()
        recv_slot(wbuf.at[block(n), pl.ds(piece, piece)], wr.at[n]).wait()

    def first(f):
        xloads[f].wait()
        xin[f].wait_recv()
        turn(f)

    def start(f):
        for direction in range(2):
            if f == 0:
                wait_w(2 * direction)
                wait_w(2 * direction + 1)
            group(f, wrap(pos[f][0] + 2), 2 * direction, 2 * direction + 2)
            for c in range(chunks):
                send_m(f, c, direction, 0)

    first(0)
    start(0)
    for copy in pin:
        copy.wait_recv()
    pin = [
        send(pf.at[pb, :, share], pf.at[pb, :, share], c1s.at[2 + o], c1r.at[2 + o], bpeer[o]) for o in (2, 1, 3)
    ]
    first(1)
    for n in range(N, 2 * N - 1):
        wait_w(n)
    start(1)

    def greet(n):
        for to in (zpeer[1], zpeer[zs - 1]):
            pl.semaphore_signal(met.at[n], inc=1, device_id=to, device_id_type=pl.DeviceIdType.MESH)

    greet(0)
    def send_m2(f, c):
        for direction in range(2):
            send_m(f, c, direction, 1)

    for i, o in enumerate((1, 3)):
        for n in range(2 * N - 1 + 3 * i, 2 * N + 2 + 3 * i):
            wait_w(n)
        both(3, lambda n: o, lambda n: N - 1 + n)
        lax.fori_loop(0, 1, single(0, lambda n: o + n), 0)
        send_m(0, 0, i, 1)
        if i == 0:
            for copy in pin:
                copy.wait_recv()
            pair = {"item": zi + 1 - 2 * lax.rem(zi, 2)}
            for j in range(N):
                send(pf.at[j, :, share], pf.at[j, :, share], c1s.at[6 + j], c1r.at[6 + j], pair)
    for n in range(N * N - 3, N * N):
        wait_w(n)
    for i, o in enumerate((1, 3)):
        both(1, lambda n: n, lambda n: o + n)
        lax.fori_loop(0, 1, single(1, lambda n: o + n), 0)
        send_m(1, 0, i, 1)

    def middle(f, c):
        for direction in range(2):
            wait_m(f, c, direction, 0)
            i1 = wrap(pos[f][0] + (1 if direction == 0 else N - 1))
            at = (f, pl.ds(i1 * N + 2 * direction, 2), slice(None), pl.ds(c * tc, tc), slice(None))
            tb[at] = (tb[at].astype(F32) + r1[f, c, direction, 0].astype(F32)).astype(BF16)
            send_m(f, c, direction, 2)

    for f in range(2):
        middle(f, 0)
        send_m2(f, 1)
    both(1, lambda n: n, lambda n: n)
    for f in range(2):
        lax.fori_loop(0, 1, single(f, lambda n: n), 0)
    for f in range(2):
        middle(f, 1)
        send_m2(f, 2)

    pl.semaphore_wait(met.at[0], 2)
    greet(1)

    theirs = pl.ds(pl.multiple_of((1 - lax.rem(zi, 2)) * 32, 32), 32)
    for i in range(piece // 64):
        at = slice(i * 64, (i + 1) * 64)
        ybuf[at, :] = dot(eye[0:64, 0:64], avp[:, at], NT)
    ybuf[piece:, :] = jnp.zeros((piece, lanes), F32)
    gram[0] = jnp.zeros((64, lanes), F32)

    def project(j, carry):
        acc, g = 0.0, 0.0
        recv_slot(pf.at[j, :, theirs], c1r.at[6 + j]).wait()
        for i in range(N):
            p = pf[j, i]
            acc = acc + dot(wbuf[index(i, j, core)], p, NT)
            g = g + dot(p[0:64], p, NT)
        ybuf[...] = ybuf[...] + acc
        gram[0] = gram[0] + g
        return carry

    lax.fori_loop(0, N, project, 0)
    yx = [
        send(ybuf.at[pl.ds(s * piece, piece)], yin.at[pl.ds((1 - s) * piece, piece)], c2s.at[33 + s], c2r.at[33 + s], sibling)
        for s in range(2)
    ]
    gin = send(gram.at[0], gram.at[1], c2s.at[1], c2r.at[1], sibling)
    for f in range(2):
        middle(f, 2)
    other = pl.multiple_of((1 - core) * half, half)
    mine = pl.multiple_of(core * half, half)
    rload.wait()
    lbuf[...] = dot(rbuf[...], pown[...], NT)
    lin = send(lbuf.at[pl.ds(other, half)], la, c2s.at[0], c2r.at[0], sibling)

    def stage2(f, c):
        wait_m(f, c, 0, 1)
        wait_m(f, c, 1, 1)
        wait_m(f, c, 0, 2)
        wait_m(f, c, 1, 2)
        for part in range(2):
            at = (f, pl.ds(pos[f][0] * N + 2 * part, 2), slice(None), pl.ds(c * tc, tc), slice(None))
            tb[at] = (
                tb[at].astype(F32)
                + r1[f, c, part, 2].astype(F32)
                + r1[f, c, 1 - part, 1].astype(F32)
            ).astype(BF16)
        for msg in range(2):
            for direction in range(2):
                send_n(f, c, direction, msg)

    def stage3(f, c):
        for direction in range(2):
            wait_n(f, c, direction, 0)
            i2 = wrap(pos[f][1] + (1 if direction == 0 else N - 1))
            at = (f, pos[f][0] * N + i2, direction, pl.ds(c * tc, tc), slice(None))
            tb[at] = (tb[at].astype(F32) + r2[f, c, direction, 0].astype(F32)).astype(BF16)
            send_n(f, c, direction, 2)

    pl.semaphore_wait(met.at[1], 2)
    greet(2)

    for copy in yx:
        copy.wait_recv()
    lin.wait_recv()
    total = lbuf[pl.ds(mine, half), :] + la[...]
    for part in split3(ybuf[...] + yin[...]):
        total = total + dot(xbuf[pl.ds(mine, half), :], part)
    lc[...] = total
    q = half // (N * N)

    def part_of(o):
        return pl.ds(pl.multiple_of((wrap(px + o[0]) * N + wrap(py + o[1])) * q, q), q)

    bins = [send(lc.at[part_of(o)], lx.at[i], c2s.at[2 + i], c2r.at[2 + i], away(o)) for i, o in enumerate(same)]
    stage2(0, 0)
    stage2(1, 0)
    stage2(0, 1)
    stage2(1, 1)
    total = lc[part_of((0, 0)), :]
    for i, copy in enumerate(bins):
        copy.wait_recv()
        total = total + lx[i]
    lfull[core, px, py] = total
    own = lfull.at[core, px, py]
    dins = [send(own, own, c2s.at[17 + i], c2r.at[17 + i], away(o)) for i, o in enumerate(same)]
    stage3(0, 0)
    stage3(1, 0)
    stage2(0, 2)
    stage2(1, 2)
    stage3(0, 1)
    stage3(1, 1)
    stage3(0, 2)
    for copy in dins:
        copy.wait_recv()
    own = lfull.at[core]
    fin = send(own, own, c2s.at[32], c2r.at[32], sibling)
    stage3(1, 2)
    pl.semaphore_wait(met.at[2], 2)
    fin.wait_recv()
    gin.wait_recv()

    low = lfull[...].reshape(rows, lanes)
    lt = low.T
    gm = (gram[0] + gram[1])[:, 0:64]
    xa = lt[64:64 + rank]
    xv = [lt[64 + rank * (i + 1):64 + rank * (i + 2)] for i in range(2)]
    zero16 = jnp.zeros((rank, rows), F32)
    hp = lt[0:64] + SCALE * dot(gm, jnp.concatenate([xa, zero16, zero16, zero16], 0), precision=HI)
    hb = hp[0:rank]
    hg = hp[48:56] + hp[56:64]
    gm8 = gm[48:56] + gm[56:64]
    stacks = [
        jnp.concatenate([xv[0], xa, zero16, zero16], 0),
        jnp.concatenate([xv[1], zero16, xa, zero16], 0),
    ]
    dhg = [SCALE * dot(gm8, st, precision=HI) for st in stacks]
    mk = [
        SCALE / model * jnp.sum(xv[i] * hb + xa * hp[rank * (i + 1):rank * (i + 2)], 0, keepdims=True)
        for i in range(2)
    ]
    prior = jnp.concatenate([prior_ref[...], jnp.zeros((4, rows), F32)], 0)

    xa_cols = [part for part in split3(low)]
    shift = (
        lax.broadcasted_iota(jnp.int32, (lanes, rank), 0) == lax.broadcasted_iota(jnp.int32, (lanes, rank), 1) + 64
    ).astype(F32).astype(BF16)
    spread = dot(shift, b_ref[...]).astype(BF16)
    ssend[...] = jnp.zeros_like(ssend)
    for c in range(chunks):
        for f in range(2):
            for direction in range(2):
                wait_n(f, c, direction, 1)
                wait_n(f, c, direction, 2)
            at = slice(f * half + c * tc, f * half + (c + 1) * tc)
            ad = dot(xa_cols[0][at], spread) + dot(xa_cols[1][at], spread) + dot(xa_cols[2][at], spread)
            parts = []
            for part in range(2):
                parts.append(
                    tb[f, pos[f][0] * N + pos[f][1], part, c * tc:(c + 1) * tc, :].astype(F32)
                    + r2[f, c, part, 2].astype(F32)
                    + r2[f, c, 1 - part, 1].astype(F32)
                )
            h = jnp.concatenate(parts, 1) + rbuf[at, :].astype(F32) + SCALE * ad
            hi = h.astype(BF16)
            hhi[at, :] = hi
            hlo[at, :] = (h - hi.astype(F32)).astype(BF16)
            sq = h * h
            sq = sq[:, :lanes] + sq[:, lanes:]
            n = f * chunks + c
            ssend[n:n + 1, :] = jnp.sum(sq.T, 0, keepdims=True)

    ins = [send(ssend, sx.at[i], c3s.at[i], c3r.at[i], away(o)) for i, o in enumerate(plane)]
    for copy in sends[:-len(ins)]:
        copy.wait_send()
    late = len(sends) - len(ins)
    stot = ssend[...]
    for i, copy in enumerate(ins):
        copy.wait_recv()
        stot = stot + sx[i]
    square = jnp.concatenate([stot[i:i + 1, :] for i in range(2 * chunks)], 1)

    r = lax.rsqrt(square / model + EPS)
    r3 = r * r * r
    live = lax.broadcasted_iota(jnp.int32, (8, rows), 0) < 4
    logits = jnp.where(live, r * hg + prior, -1e30)
    ex = jnp.where(live, jnp.exp(logits - jnp.max(logits, 0, keepdims=True)), 0.0)
    p = ex / jnp.sum(ex, 0, keepdims=True)
    us, cs, t1 = [], [], []
    gcol = gm[0:rank]
    for i in range(2):
        dl = r * dhg[i] - r3 * mk[i] * hg
        q = p * (dl - jnp.sum(p * dl, 0, keepdims=True)) / total_tokens
        s = jnp.sum(q * hg, 0, keepdims=True) / model
        back = dot(gcol, jnp.concatenate([zero16, zero16, zero16, q, q], 0), precision=HI)
        us.append(SCALE * (r * back - r3 * s * hb))
        cs.append(r3 * s * xa)
        t1.append(dot(xa, r * q, NT, precision=HI))
    uu = jnp.concatenate(split3(jnp.concatenate(us, 0)), 0)
    cc = jnp.concatenate(split3(jnp.concatenate(cs, 0)), 0)
    n32 = 2 * rank

    def fold(m):
        return m[0:n32] + m[n32:2 * n32] + m[2 * n32:3 * n32]

    ggn = fold(dot(uu, xbuf[:, 0:piece]))
    ch = fold(dot(cc, hhi[...]) + dot(cc, hlo[...]))
    curv = SCALE * (dot(jnp.concatenate(t1, 0), g8[...], precision=HI) - ch)

    zw = 3 * lanes
    for i in range(4):
        at = slice(8 * i, 8 * i + 8)
        zpart[2 * i] = ggn[at, 0:zw]
        zpart[2 * i + 1, :, 0:piece - zw] = ggn[at, zw:piece]
        zpart[2 * i + 1, :, lanes:zw] = curv[at, :]
    ins = []
    for o in zorder:
        ins.append(send(zpart.at[lax.rem(zi + o, zs)], zrecv.at[o - 1], zss.at[0, o - 1], zsr.at[0, o - 1], zpeer[o]))
    for copy in ins:
        copy.wait_recv()
    total = zpart[zi]
    for o in range(1, zs):
        total = total + zrecv[o - 1]
    zfull[zi] = total
    ins = [
        send(zfull.at[zi], zfull.at[zi], zss.at[1, o - 1], zsr.at[1, o - 1], zpeer[o]) for o in zorder
    ]
    for copy in ins:
        copy.wait_recv()
    out_ref[...] = zfull[...]
    for copy in sends[late:]:
        copy.wait_send()


def unpack(in_ref, ggn_ref, curv_ref):
    zw = in_ref.shape[2]
    piece = ggn_ref.shape[1]
    for i in range(4):
        at = slice(8 * i, 8 * i + 8)
        ggn_ref[at, 0:zw] = in_ref[2 * i]
        ggn_ref[at, zw:piece] = in_ref[2 * i + 1, :, 0:piece - zw]
        curv_ref[at, :] = in_ref[2 * i + 1, :, 128:zw]


def shards(zs, x, res, w, a_in, b_out, gain, head, prior, v_in, d_out):
    rows, piece = x.shape
    fb = res.shape[1]
    rank = a_in.shape[0]
    k = v_in.shape[0]
    chunks = 3
    half = rows // 2
    tc = half // chunks
    q = half // N // N
    vmem = pl.BlockSpec(memory_space=pltpu.VMEM)
    hbm = pl.BlockSpec(memory_space=pl.ANY)
    dma = pltpu.SemaphoreType.DMA
    packed = pl.pallas_call(
        functools.partial(kernel, chunks, zs, rows * zs),
        out_shape=jax.ShapeDtypeStruct((8, 8, 384), F32),
        in_specs=[hbm] * 10,
        out_specs=vmem,
        scratch_shapes=[
            pltpu.VMEM(a_in.shape, BF16),
            pltpu.VMEM(b_out.shape, BF16),
            pltpu.VMEM(gain.shape, BF16),
            pltpu.VMEM(head.shape, BF16),
            pltpu.VMEM((prior.shape[1], rows), F32),
            pltpu.VMEM((k * rank, piece), BF16),
            pltpu.VMEM((k * rank, fb), BF16),
            dma((7,)),
            pltpu.VMEM((2 * piece, rows), BF16),
            pltpu.VMEM((rows, 2 * piece), BF16),
            pltpu.VMEM((rows, fb), BF16),
            pltpu.VMEM((N * N, 2 * piece, fb), BF16),
            pltpu.VMEM((2, N * N, 2, half, 128), BF16),
            pltpu.VMEM((2, chunks, 2, 3, 2, 2, tc, 128), BF16),
            pltpu.VMEM((2, chunks, 2, 3, tc, 128), BF16),
            pltpu.VMEM((N, N, 128, fb), BF16),
            pltpu.VMEM((128, fb), BF16),
            pltpu.VMEM((8, fb), F32),
            pltpu.VMEM((128, piece), BF16),
            pltpu.VMEM((2 * piece, 128), F32),
            pltpu.VMEM((2 * piece, 128), F32),
            pltpu.VMEM((2, 64, 128), F32),
            pltpu.VMEM((rows, 128), F32),
            pltpu.VMEM((half, 128), F32),
            pltpu.VMEM((half, 128), F32),
            pltpu.VMEM((N * N - 1, q, 128), F32),
            pltpu.VMEM((2, N, N, q, 128), F32),
            pltpu.VMEM((rows, fb), BF16),
            pltpu.VMEM((rows, fb), BF16),
            pltpu.VMEM((8, 128), F32),
            pltpu.VMEM((2 * N * N - 1, 8, 128), F32),
            pltpu.VMEM((8, 8, 384), F32),
            pltpu.VMEM((zs - 1, 8, 384), F32),
            pltpu.VMEM((8, 8, 384), F32),
            dma((N * N,)), dma((2,)), dma((1,)),
            dma((N * N,)), dma((N * N,)), dma((2,)), dma((2,)),
            dma((2, chunks, 2, 3)), dma((2, chunks, 2, 3)),
            dma((2, chunks, 2, 3)), dma((2, chunks, 2, 3)),
            dma((10,)), dma((10,)),
            dma((35,)), dma((35,)), dma((2 * N * N - 1,)), dma((2 * N * N - 1,)),
            dma((2, zs - 1)), dma((2, zs - 1)),
            pltpu.SemaphoreType.REGULAR((3,)),
        ],
        compiler_params=pltpu.CompilerParams(
            collective_id=0, has_side_effects=True, vmem_limit_bytes=56 * 1024 * 1024
        ),
    )(
        x.T, res, w, a_in, b_out, gain, head, prior.T,
        v_in.reshape(k * rank, piece), d_out.reshape(k * rank, fb),
    )
    ggn, curv = pl.pallas_call(
        unpack,
        out_shape=(
            jax.ShapeDtypeStruct((k * rank, piece), F32),
            jax.ShapeDtypeStruct((k * rank, fb), F32),
        ),
    )(packed)
    return ggn.reshape(k, rank, piece), curv.reshape(k, rank, fb)


def solution(mesh):
    placed = (
        P("item", "tensor"),
        P("item", "tensor"),
        P("tensor", None),
        P(None, "tensor"),
        P(None, "tensor"),
        P("tensor"),
        P(None, "tensor"),
        P("item", None),
        P(None, None, "tensor"),
        P(None, None, "tensor"),
    )
    return jax.shard_map(
        functools.partial(shards, mesh.shape["item"]),
        mesh=mesh,
        in_specs=placed,
        out_specs=(P(None, None, "tensor"), P(None, None, "tensor")),
        check_vma=False,
    )
```
